256 devices in a mesh: trow: 32 (over z, x_lo, core), tcol: 8 (over x_hi, y).
Axes of the slice: x: 4 (x_hi: 2, x_lo: 2; x = x_hi * 2 + x_lo), y: 4, z: 8, core: 2. Of those that a mesh axis runs over, the one named last changes fastest.
Arguments:
- lesser: bfloat16 [2, 3072, 3072], P(None, 'trow', 'tcol'), may hold values from -4 to 4
- greater: bfloat16 [2, 3072, 3072], P(None, 'trow', 'tcol'), may hold values from -4 to 4
- hopping: bfloat16 [32, 32], replicated, may hold values from -1 to 1
- coupling: float32 [32], replicated, may hold values from 0.5 to 1.5
Outputs:
- lesser_out: bfloat16 [2, 3072, 3072], P(None, 'trow', 'tcol')
- greater_out: bfloat16 [2, 3072, 3072], P(None, 'trow', 'tcol')
The draws below stay inside these ranges and needn't reach their ends.
All inputs are finite; a program needn't handle non-finite values.
Results may differ from the reference program's by a relative error of at most 0.0068.
Values may be sent and summed in bfloat16 or wider, within the bound.
A program may use at most 64 MiB of HBM per device.

```python
import math
import jax
import jax.numpy as jnp

ORBITAL_COUNT = 32
STEPS = 2
WINDOW_TIMES = 96


def steps_of(rng, extent, pieces, low, largest):
    level, own = 1.0, jax.random.fold_in(rng, 6)
    for dim, parts in pieces:
        draws = jnp.exp(jax.random.uniform(jax.random.fold_in(own, dim), (parts,), jnp.float32, low / len(pieces), largest / len(pieces)))
        level = level * jnp.repeat(draws, extent[dim] // parts).reshape([-1 if axis == dim else 1 for axis in range(len(extent))])
    return level


def gaussian(own_key, dims, spread, limit, shards=(), held_as=jnp.bfloat16):
    result = spread * jax.random.normal(own_key, dims, jnp.float32)
    if shards:
        result = result * steps_of(own_key, dims, shards, -0.22, 0.18)
    return jnp.clip(result, -limit, limit).astype(held_as)


def setup_inputs(seed: int = 0) -> dict:
    streams_of = jax.random.split(jax.random.key(seed), 5)
    lesser = gaussian(streams_of[0], (2, WINDOW_TIMES * ORBITAL_COUNT, WINDOW_TIMES * ORBITAL_COUNT), 0.6, 4.0, ((1, 32), (2, 8)))
    greater = gaussian(streams_of[1], (2, WINDOW_TIMES * ORBITAL_COUNT, WINDOW_TIMES * ORBITAL_COUNT), 0.6, 4.0, ((1, 32), (2, 8)))
    hopping = gaussian(streams_of[2], (ORBITAL_COUNT, ORBITAL_COUNT), ORBITAL_COUNT ** -0.5, 1.0)
    coupling = jnp.clip(jnp.exp(jax.random.uniform(streams_of[3], (ORBITAL_COUNT,), jnp.float32, math.log(0.5), math.log(1.5))), 0.5, 1.5)
    return {"lesser": lesser, "greater": greater, "hopping": hopping, "coupling": coupling}


def pair_energy(factor, partner, weights):
    base_r = factor[0].astype(jnp.float32)
    base_i = factor[1].astype(jnp.float32)
    mirror_r = partner[0].T.astype(jnp.float32)
    mirror_i = partner[1].T.astype(jnp.float32)
    square_r = base_r * base_r - base_i * base_i
    square_i = 2.0 * base_r * base_i
    scaling = weights[:, None] * weights[None, :]
    real_part = (square_r * mirror_r - square_i * mirror_i) * scaling
    imag_part = (square_r * mirror_i + square_i * mirror_r) * scaling
    return jnp.stack([real_part, imag_part]).astype(jnp.bfloat16)


def matmul_f32(left_op, right_op):
    return jnp.dot(left_op, right_op, preferred_element_type=jnp.float32)


def complex_product(left_op, right_op):
    real_part = matmul_f32(left_op[0], right_op[0]) - matmul_f32(left_op[1], right_op[1])
    imag_part = matmul_f32(left_op[0], right_op[1]) + matmul_f32(left_op[1], right_op[0])
    return real_part, imag_part


def advance_step(current_state, boundary_rows, collision_real, collision_imaginary, hopping, time_increment):
    window_width = WINDOW_TIMES * ORBITAL_COUNT
    blocks = current_state.reshape(2, WINDOW_TIMES, ORBITAL_COUNT, window_width).astype(jnp.float32)
    hopping_applied = jnp.einsum('ik,ctkx->ctix', hopping.astype(jnp.float32), blocks)
    derivative_real = hopping_applied[1] + collision_imaginary.reshape(WINDOW_TIMES, ORBITAL_COUNT, window_width)
    derivative_imaginary = -(hopping_applied[0] + collision_real.reshape(WINDOW_TIMES, ORBITAL_COUNT, window_width))
    rates = jnp.stack([derivative_real, derivative_imaginary])
    summed = jnp.cumsum(rates, axis=1)
    before = jnp.concatenate([jnp.zeros((2, 1, ORBITAL_COUNT, window_width), jnp.float32), summed[:, :-1]], axis=1)
    renewed = boundary_rows.astype(jnp.float32)[:, None] + time_increment * before
    return renewed.reshape(2, window_width, window_width).astype(jnp.bfloat16)


def reference(lesser, greater, hopping, coupling):
    time_increment = 3.0 / WINDOW_TIMES
    weights = jnp.tile(coupling, WINDOW_TIMES)
    boundary_lesser = lesser[:, :ORBITAL_COUNT, :]
    boundary_greater = greater[:, :ORBITAL_COUNT, :]
    current_lesser = lesser
    current_greater = greater
    for sweep in range(STEPS):
        sigma_less = pair_energy(current_lesser, current_greater, weights)
        sigma_great = pair_energy(current_greater, current_lesser, weights)
        greater_real, greater_imaginary = complex_product(sigma_great, current_lesser)
        lesser_real, lesser_imaginary = complex_product(sigma_less, current_greater)
        collision_real = time_increment * (greater_real - lesser_real)
        collision_imaginary = time_increment * (greater_imaginary - lesser_imaginary)
        following_lesser = advance_step(current_lesser, boundary_lesser, collision_real, collision_imaginary, hopping, time_increment)
        following_greater = advance_step(current_greater, boundary_greater, collision_real, collision_imaginary, hopping, time_increment)
        current_lesser = following_lesser
        current_greater = following_greater
    return current_lesser, current_greater
```

```python
import functools

import jax
import jax.numpy as jnp
from jax import lax
from jax.experimental import pallas as pl
from jax.experimental.pallas import tpu as pltpu
from jax.sharding import PartitionSpec as P

MESH = pl.DeviceIdType.MESH
ORB = 32
STEPS = 2
N = 8
Q = 4
Y = 4
F32 = jnp.float32
BF16 = jnp.bfloat16
NT = (((1,), (1,)), ((), ()))
NN = (((1,), (0,)), ((), ()))


def dot(a, b, dims=NN):
    return lax.dot_general(a, b, dims, preferred_element_type=F32)


def kernel(
    dt, x, w, h3, out,
    xq, t1, t2, f, sg, hb, acc, bm, rs_s, rs_r, zt_s, zt_r, ax_s, ax_r, ed_r, a_s, a_r,
    s_t1, r_t1, s_t2, r_t2, s_t3, r_t3, s_q, r_q, s_h, r_h, s_s, r_s,
    s_rs, r_rs, s_zt, r_zt, s_ax, r_ax, s_ed, r_ed, s_a, r_a,
):
    rows = x.shape[1]
    cols = x.shape[2]
    times = rows // ORB
    half = rows // 2
    r = lax.axis_index("trow")
    b = lax.axis_index("tcol")
    z, q = r // Q, r % Q
    xh, y = b // Y, b % Y

    def at_z(zz):
        return {"trow": zz * Q + q, "tcol": b}

    def at_q(qq):
        return {"trow": z * Q + qq, "tcol": b}

    def at_b(bb):
        return {"trow": r, "tcol": bb}

    started = []

    def send(src, dst, ss, rs, where):
        copy = pltpu.make_async_remote_copy(
            src_ref=src, dst_ref=dst, send_sem=ss, recv_sem=rs, device_id=where, device_id_type=MESH
        )
        copy.start()
        return copy

    def push(src, dst, ss, rs, where):
        started.append(send(src, dst, ss, rs, where))

    def arrive(dst, ss, rs):
        pltpu.make_async_remote_copy(
            src_ref=dst, dst_ref=dst, send_sem=ss, recv_sem=rs, device_id=at_b(b), device_id_type=MESH
        ).wait_recv()

    def sent(src, ss, rs):
        pltpu.make_async_remote_copy(
            src_ref=src, dst_ref=src, send_sem=ss, recv_sem=rs, device_id=at_b(b), device_id_type=MESH
        ).wait_send()

    def slab(p):
        return x.at[p // 2, pl.ds(pl.multiple_of(half * (p % 2), half), half)]

    barrier = pltpu.get_barrier_semaphore()
    for i in range(1, N):
        pl.semaphore_signal(barrier, inc=1, device_id=at_b((b + i) % N), device_id_type=MESH)
        pl.semaphore_signal(barrier, inc=1, device_id=at_z((z + i) % N), device_id_type=MESH)
    for i in range(1, Q):
        pl.semaphore_signal(barrier, inc=1, device_id=at_q((q + i) % Q), device_id_type=MESH)
    pl.semaphore_wait(barrier, 2 * (N - 1) + Q - 1)

    for i in range(1, N):
        p = (b + i) % N
        push(slab(p), t1.at[b], s_t1.at[i], r_t1.at[i], at_b(p))
    sib = (q // 2) * 2 + (1 - q % 2)
    par = (q + 2) % Q
    push(x, xq.at[:, q], s_q.at[0], r_q.at[0], at_q(sib))
    push(x, xq.at[:, q], s_q.at[1], r_q.at[1], at_q(par))
    t1[b] = slab(b)[...]
    xq[:, q] = x[...]
    hb[z] = x[...]

    for i in range(N):
        bb = (b + N - i) % N
        if i > 0:
            arrive(t1.at[bb], s_t1.at[i], r_t1.at[i])
        j = (bb + N - z) % N

        @pl.when(j != 0)
        def _():
            send(t1.at[bb], t2.at[z], s_t2.at[j], r_t2.at[j], at_z(bb))

        @pl.when(j == 0)
        def _():
            t2[z] = t1[bb]

    up, down = at_z((z + 1) % N), at_z((z + N - 1) % N)
    push(x, hb.at[z], s_h.at[0], r_h.at[0], up)
    push(x, hb.at[z], s_h.at[1], r_h.at[1], down)

    def pass_history(step):
        lo = hb.at[(z + N - step) % N]
        hi = hb.at[(z + step) % N]
        if step < 4:
            arrive(lo, s_h.at[2 * step - 2], r_h.at[2 * step - 2])
            arrive(hi, s_h.at[2 * step - 1], r_h.at[2 * step - 1])
        else:
            first, second = lo.at[pl.ds(0, 2)], hi.at[pl.ds(2, 2)]
            arrive(first, s_h.at[2 * step - 2], r_h.at[2 * step - 2])
            arrive(second, s_h.at[2 * step - 1], r_h.at[2 * step - 1])
            return
        if step < 3:
            push(lo, lo, s_h.at[2 * step], r_h.at[2 * step], up)
            push(hi, hi, s_h.at[2 * step + 1], r_h.at[2 * step + 1], down)
        else:
            push(lo.at[pl.ds(0, 2)], lo.at[pl.ds(0, 2)], s_h.at[6], r_h.at[6], up)
            push(hi.at[pl.ds(2, 2)], hi.at[pl.ds(2, 2)], s_h.at[7], r_h.at[7], down)

    for i in range(N):
        zz = (z + N - i) % N
        if i > 0:
            arrive(t2.at[zz], s_t2.at[i], r_t2.at[i])
        j = (zz + N - b) % N

        @pl.when(j != 0)
        def _():
            send(t2.at[zz], f.at[b], s_t3.at[j], r_t3.at[j], at_b(zz))

        @pl.when(j == 0)
        def _():
            f[b] = t2[zz]

    arrive(xq.at[:, par], s_q.at[1], r_q.at[1])
    push(xq.at[:, par], xq.at[:, par], s_q.at[2], r_q.at[2], at_q(sib))
    arrive(xq.at[:, sib], s_q.at[0], r_q.at[0])
    arrive(xq.at[:, (sib + 2) % Q], s_q.at[2], r_q.at[2])

    one_hot = (
        lax.broadcasted_iota(jnp.int32, (rows, cols), 1)
        == lax.broadcasted_iota(jnp.int32, (rows, cols), 0) + rows * q
    ).astype(F32).astype(BF16)
    base = [dot(one_hot, xq[c].reshape(cols, cols), NT) for c in range(4)]
    for i in range(1, N):
        p = (b + N - i) % N
        arrive(f.at[p], s_t3.at[i], r_t3.at[i])
    mirror = f[...].reshape(4, rows, cols).astype(F32)
    weight = w[...]

    def energy(br, bi, mr, mi):
        sr = br * br - bi * bi
        si = 2.0 * br * bi
        return [((sr * mr - si * mi) * weight).astype(BF16), ((sr * mi + si * mr) * weight).astype(BF16)]

    parts = energy(base[2], base[3], mirror[0], mirror[1]) + energy(base[0], base[1], mirror[2], mirror[3])
    sigma = jnp.concatenate(parts, axis=0)
    eye = (
        lax.broadcasted_iota(jnp.int32, (cols, cols), 1) == lax.broadcasted_iota(jnp.int32, (cols, cols), 0)
    ).astype(F32).astype(BF16)
    sg[b] = dot(eye, sigma, NT).astype(BF16)

    def place(dx, dy):
        return ((xh + dx) % 2) * Y + (y + dy) % Y

    nxt, prv, opp = place(0, 1), place(0, 3), place(1, 0)

    def share(src_place, k):
        push(sg.at[src_place], sg.at[src_place], s_s.at[k], r_s.at[k], at_b(nxt))
        push(sg.at[src_place], sg.at[src_place], s_s.at[k + 1], r_s.at[k + 1], at_b(prv))

    def share_far(dx, k):
        before, after = place(dx, 3), place(dx, 1)
        arrive(sg.at[before], s_s.at[k], r_s.at[k])
        one = sg.at[before, pl.ds(0, cols // 2)]
        push(one, one, s_s.at[k + 2], r_s.at[k + 2], at_b(nxt))
        arrive(sg.at[after], s_s.at[k + 1], r_s.at[k + 1])
        two = sg.at[after, pl.ds(cols // 2, cols // 2)]
        push(two, two, s_s.at[k + 3], r_s.at[k + 3], at_b(prv))

    def arrive_far(dx, k):
        far = place(dx, 2)
        arrive(sg.at[far, pl.ds(0, cols // 2)], s_s.at[k + 2], r_s.at[k + 2])
        arrive(sg.at[far, pl.ds(cols // 2, cols // 2)], s_s.at[k + 3], r_s.at[k + 3])

    push(sg.at[b], sg.at[b], s_s.at[0], r_s.at[0], at_b(opp))
    share(b, 1)
    pass_history(1)
    arrive(sg.at[opp], s_s.at[0], r_s.at[0])
    share(opp, 5)
    pass_history(2)
    share_far(0, 1)
    pass_history(3)
    share_far(1, 5)
    pass_history(4)

    before = jnp.zeros((4, ORB, cols), F32)
    for zz in range(N - 1):
        tile = hb[zz].astype(F32)
        total = tile[:, 0:ORB]
        for k in range(1, times):
            total = total + tile[:, k * ORB:(k + 1) * ORB]
        before = before + jnp.where(zz < z, total, 0.0)
    ax_s[...] = before.astype(BF16)
    for i in range(1, Q):
        push(ax_s, ax_r.at[q], s_ax.at[i], r_ax.at[i], at_q((q + i) % Q))

    @pl.when(q == 0)
    def _():
        edge = hb[0, :, 0:ORB]
        ed_r[...] = edge
        for i in range(1, Q):
            send(hb.at[0, :, pl.ds(0, ORB)], ed_r, s_ed.at[i], r_ed.at[0], at_q(i))

    def multiply(bb, first):
        tile = hb[bb]
        lr, li, gr, gi = tile[0], tile[1], tile[2], tile[3]
        bm[:, 0:cols] = jnp.concatenate([lr, -li, -gr, gi], axis=0)
        bm[:, cols:2 * cols] = jnp.concatenate([li, lr, -gi, -gr], axis=0)
        prod = dot(sg[bb], bm[...])
        if first:
            acc[...] = prod
        else:
            acc[...] += prod

    multiply(b, True)
    multiply(opp, False)
    multiply(prv, False)
    multiply(nxt, False)
    multiply(place(1, 3), False)
    multiply(place(1, 1), False)
    arrive_far(0, 1)
    multiply(place(0, 2), False)
    arrive_far(1, 5)
    multiply(place(1, 2), False)

    run = jnp.zeros((ORB, 2 * cols), F32)
    for k in range(Q):
        for m in range(times):
            at = (k * times + m) * ORB
            term = acc[pl.ds(at, ORB), :]
            acc[pl.ds(at, ORB), :] = run
            rs_s[k, pl.ds(m * ORB, ORB), :] = run.astype(BF16)
            run = run + term
    zt_s[...] = run.astype(BF16)
    for i in range(1, N):
        @pl.when(z + i < N)
        def _():
            send(zt_s, zt_r.at[z], s_zt.at[i], r_zt.at[i], at_z(z + i))
    for i in range(1, Q):
        to = (q + i) % Q
        push(rs_s.at[to], rs_r.at[q], s_rs.at[i], r_rs.at[i], at_q(to))

    carry = jnp.zeros((ORB, 2 * cols), F32)
    for i in range(1, N):
        @pl.when(z - i >= 0)
        def _():
            arrive(zt_r.at[z - i], s_zt.at[i], r_zt.at[i])
    for zz in range(N - 1):
        carry = carry + jnp.where(zz < z, zt_r[zz].astype(F32), 0.0)
    a_s[...] = carry.astype(BF16)
    for i in range(1, Q):
        push(a_s, a_r.at[q], s_a.at[i], r_a.at[i], at_q((q + i) % Q))

    for i in range(1, Q):
        arrive(ax_r.at[(q + Q - i) % Q], s_ax.at[i], r_ax.at[i])
        before = before + ax_r[(q + Q - i) % Q].astype(F32)

    @pl.when(q != 0)
    def _():
        arrive(ed_r, s_ed.at[0], r_ed.at[0])

    for qq in range(Q - 1):
        tile = xq[:, qq].astype(F32)
        total = tile[:, 0:ORB]
        for k in range(1, times):
            total = total + tile[:, k * ORB:(k + 1) * ORB]
        before = before + jnp.where(qq < q, total, 0.0)
    own = x[...].astype(F32)
    hopped = []
    hop = h3[...]
    for c in range(4):
        level = before[c]
        levels = [level]
        for k in range(times - 1):
            level = level + own[c, k * ORB:(k + 1) * ORB]
            levels.append(level)
        level = jnp.concatenate(levels, axis=0)
        high = level.astype(BF16)
        low = (level - high.astype(F32)).astype(BF16)
        hopped.append(dot(hop, high) + dot(hop, low))

    coll = acc[pl.ds(pl.multiple_of(q * rows, rows), rows), :]
    for i in range(1, Q):
        arrive(rs_r.at[(q + Q - i) % Q], s_rs.at[i], r_rs.at[i])
        coll = coll + rs_r[(q + Q - i) % Q].astype(F32)
    for i in range(1, Q):
        arrive(a_r.at[(q + Q - i) % Q], s_a.at[i], r_a.at[i])
        carry = carry + a_r[(q + Q - i) % Q].astype(F32)
    coll = dt * (coll + jnp.concatenate([carry] * times, axis=0))
    for c in range(4):
        edge = jnp.concatenate([ed_r[c].astype(F32)] * times, axis=0)
        if c % 2 == 0:
            new = edge + dt * (hopped[c + 1] + coll[:, cols:])
        else:
            new = edge - dt * (hopped[c - 1] + coll[:, :cols])
        out[c] = new.astype(BF16)

    for copy in started:
        copy.wait_send()
    for i in range(N):
        bb = (b + N - i) % N
        j = (bb + N - z) % N

        @pl.when(j != 0)
        def _():
            sent(t1.at[bb], s_t2.at[j], r_t2.at[j])

        zz = (z + N - i) % N
        k = (zz + N - b) % N

        @pl.when(k != 0)
        def _():
            sent(t2.at[zz], s_t3.at[k], r_t3.at[k])
    for i in range(1, N):
        @pl.when(z + i < N)
        def _():
            sent(zt_s, s_zt.at[i], r_zt.at[i])

    @pl.when(q == 0)
    def _():
        for i in range(1, Q):
            sent(hb.at[0, :, pl.ds(0, ORB)], s_ed.at[i], r_ed.at[0])


def one_step(x, w, h3, dt):
    rows, cols = x.shape[1:]
    dma = pltpu.SemaphoreType.DMA
    sems = [8, 8, 8, 8, 8, 8, 3, 3, 8, 8, 9, 9, 4, 4, 8, 8, 4, 4, 4, 1, 4, 4]
    return pl.pallas_call(
        functools.partial(kernel, dt),
        out_shape=jax.ShapeDtypeStruct(x.shape, BF16),
        in_specs=[pl.BlockSpec(memory_space=pltpu.VMEM)] * 3,
        out_specs=pl.BlockSpec(memory_space=pltpu.VMEM),
        scratch_shapes=[
            pltpu.VMEM((4, Q, rows, cols), BF16),
            pltpu.VMEM((N, rows // 2, cols), BF16),
            pltpu.VMEM((N, rows // 2, cols), BF16),
            pltpu.VMEM((N, rows // 2, cols), BF16),
            pltpu.VMEM((N, cols, cols), BF16),
            pltpu.VMEM((N, 4, rows, cols), BF16),
            pltpu.VMEM((cols, 2 * cols), F32),
            pltpu.VMEM((cols, 2 * cols), BF16),
            pltpu.VMEM((Q, rows, 2 * cols), BF16),
            pltpu.VMEM((Q, rows, 2 * cols), BF16),
            pltpu.VMEM((ORB, 2 * cols), BF16),
            pltpu.VMEM((N, ORB, 2 * cols), BF16),
            pltpu.VMEM((4, ORB, cols), BF16),
            pltpu.VMEM((Q, 4, ORB, cols), BF16),
            pltpu.VMEM((4, ORB, cols), BF16),
            pltpu.VMEM((ORB, 2 * cols), BF16),
            pltpu.VMEM((Q, ORB, 2 * cols), BF16),
        ] + [dma((n,)) for n in sems],
        compiler_params=pltpu.CompilerParams(
            collective_id=0, has_side_effects=True, vmem_limit_bytes=48 * 1024 * 1024
        ),
        cost_estimate=pl.CostEstimate(flops=2 * 4 * 768 * 768 * 768, bytes_accessed=10**6, transcendentals=0),
    )(x, w, h3)


def per_device(lesser, greater, hopping, coupling):
    rows, cols = lesser.shape[1:]
    dt = 3.0 / (rows * N * Q // ORB)
    w = jnp.tile(coupling, rows // ORB)[:, None] * jnp.tile(coupling, cols // ORB)[None, :]
    h3 = jnp.kron(jnp.eye(rows // ORB, dtype=hopping.dtype), hopping)
    x = jnp.concatenate([lesser, greater], axis=0)
    for _ in range(STEPS):
        x = one_step(x, w, h3, dt)
    return x[:2], x[2:]


def solution(mesh):
    in_specs = (P(None, "trow", "tcol"), P(None, "trow", "tcol"), P(), P())
    out_specs = (P(None, "trow", "tcol"), P(None, "trow", "tcol"))
    return jax.shard_map(per_device, mesh=mesh, in_specs=in_specs, out_specs=out_specs, check_vma=False)
```

```python
import functools

import jax
import jax.numpy as jnp
from jax import lax
from jax.experimental import pallas as pl
from jax.experimental.pallas import tpu as pltpu
from jax.sharding import PartitionSpec as P

MESH = pl.DeviceIdType.MESH
ORB = 32
STEPS = 2
N = 8
Q = 4
Y = 4
J = 3
HALF = ORB // 2
F32 = jnp.float32
BF16 = jnp.bfloat16
NT = (((1,), (1,)), ((), ()))
NN = (((1,), (0,)), ((), ()))
PIECES = ((0, 0, Q * J), (1, 0, Q * J), (2, 0, Q), (2, Q, Q), (2, 2 * Q, Q))


def dot(a, b, dims=NN):
    return lax.dot_general(a, b, dims, preferred_element_type=F32)


def kernel(
    dt, lesser, greater, w, h3, out_l, out_g,
    x, xq, t1, f, sg, hb, bm, acc, pre, hop, zs_s, zs_r, cs, rs_s, rs_r, ax_s, ax_r, ed,
    s_in, s_t1, r_t1, s_t2, r_t2, s_q, r_q, s_h, r_h, s_g, r_g,
    s_zs, r_zs, s_cs, r_cs, s_rs, r_rs, s_ax, r_ax, s_ed, r_ed,
):
    cols = x.shape[-1]
    wide = 4 * ORB
    r = lax.axis_index("trow")
    b = lax.axis_index("tcol")
    z, q = r // Q, r % Q
    xh, y = b // Y, b % Y

    def at(zz, qq, bb):
        return {"trow": zz * Q + qq, "tcol": bb}

    drains = []

    def copy_of(src, dst, ss, rs, where):
        return pltpu.make_async_remote_copy(
            src_ref=src, dst_ref=dst, send_sem=ss, recv_sem=rs, device_id=where, device_id_type=MESH
        )

    def push(src, dst, ss, rs, where):
        copy = copy_of(src, dst, ss, rs, where)
        copy.start()
        drains.append(copy.wait_send)

    def push_if(cond, src, dst, ss, rs, where):
        @pl.when(cond)
        def _():
            copy_of(src, dst, ss, rs, where).start()

        def drain():
            @pl.when(cond)
            def _():
                copy_of(src, dst, ss, rs, where).wait_send()

        drains.append(drain)

    def arrive(dst, rs):
        copy_of(dst, dst, s_in.at[0], rs, at(z, q, b)).wait_recv()

    def place(dx, dy):
        return ((xh + dx) % 2) * Y + (y + dy) % Y

    sib = (q // 2) * 2 + (1 - q % 2)
    par = (q + 2) % Q
    dia = (sib + 2) % Q
    up, down = at((z + 1) % N, q, b), at((z + N - 1) % N, q, b)


    def mirror_out(st, j):
        for i in range(1, N):
            p = (b + i) % N
            k = (st * J + j) * N + i
            src = x.at[st, p // 2, j, pl.ds(pl.multiple_of(HALF * (p % 2), HALF), HALF)]
            push(src, t1.at[st, j, b], s_t1.at[k], r_t1.at[k], at(z, q, p))
        t1[st, j, b] = x[st, b // 2, j, pl.ds(pl.multiple_of(HALF * (b % 2), HALF), HALF)]

    def mirror_on(st, j):
        base = (st * J + j) * N
        for i in range(N):
            bb = (b + N - i) % N
            if i > 0:
                arrive(t1.at[st, j, bb], r_t1.at[base + i])
            here = jnp.logical_and(bb == z, b == z)
            push_if(
                jnp.logical_not(here), t1.at[st, j, bb], f.at[st, j, b], s_t2.at[base + i], r_t2.at[base + b], at(bb, q, z)
            )

            @pl.when(here)
            def _():
                f[st, j, b] = t1[st, j, bb]

    def mirror_in(st, j):
        base = (st * J + j) * N
        for i in range(N):
            p = (b + i) % N
            if i > 0:
                arrive(f.at[st, j, p], r_t2.at[base + p])
            else:
                @pl.when(b != z)
                def _():
                    arrive(f.at[st, j, p], r_t2.at[base + p])

    def quad_out(st, j):
        k = (st * J + j) * 3
        push(x.at[st, :, j], xq.at[st, :, q, j], s_q.at[k + 1], r_q.at[k + 1], at(z, par, b))
        push(x.at[st, :, j], xq.at[st, :, q, j], s_q.at[k], r_q.at[k], at(z, sib, b))
        xq[st, :, q, j] = x[st, :, j]

    def quad_on(st, j):
        k = (st * J + j) * 3
        arrive(xq.at[st, :, par, j], r_q.at[k + 1])
        push(xq.at[st, :, par, j], xq.at[st, :, par, j], s_q.at[k + 2], r_q.at[k + 2], at(z, sib, b))

    def quad_in(st, j):
        k = (st * J + j) * 3
        arrive(xq.at[st, :, sib, j], r_q.at[k])
        arrive(xq.at[st, :, dia, j], r_q.at[k + 2])

    def history(st, s, j):
        base = (st * J + j) * 8
        lo, hi = (z + N - s) % N, (z + s) % N
        first, second = (pl.ds(0, 2), pl.ds(2, 2)) if s >= 3 else (pl.ds(0, 4), pl.ds(0, 4))
        if s > 0:
            got = (pl.ds(0, 2), pl.ds(2, 2)) if s == 4 else (pl.ds(0, 4), pl.ds(0, 4))
            arrive(hb.at[st, lo, got[0], j], r_h.at[base + 2 * s - 2])
            arrive(hb.at[st, hi, got[1], j], r_h.at[base + 2 * s - 1])
        if s < 4:
            one, two = hb.at[st, lo, first, j], hb.at[st, hi, second, j]
            from_one, from_two = (x.at[st, :, j], x.at[st, :, j]) if s == 0 else (one, two)
            push(from_one, one, s_h.at[base + 2 * s], r_h.at[base + 2 * s], up)
            push(from_two, two, s_h.at[base + 2 * s + 1], r_h.at[base + 2 * s + 1], down)

    def tile(st, piece, bb):
        k, m, n = PIECES[piece]
        return sg.at[st, k, pl.ds(ORB * (1 + m), ORB * n), pl.ds(pl.multiple_of(wide * bb, wide), wide)]

    def give(st, piece, way, bb, to):
        k = (st * len(PIECES) + piece) * 7 + way
        push(tile(st, piece, bb), tile(st, piece, bb), s_g.at[k], r_g.at[k], at(z, q, to))

    def take(st, piece, way, bb):
        arrive(tile(st, piece, bb), r_g.at[(st * len(PIECES) + piece) * 7 + way])

    def give_own(st, piece):
        give(st, piece, 0, b, place(1, 0))
        give(st, piece, 1, b, place(0, 1))
        give(st, piece, 2, b, place(0, 3))

    def give_partner(st, piece):
        take(st, piece, 0, place(1, 0))
        give(st, piece, 3, place(1, 0), place(0, 1))
        give(st, piece, 4, place(1, 0), place(0, 3))

    def give_far(st, piece):
        take(st, piece, 1, place(0, 3))
        give(st, piece, 5, place(0, 3), place(0, 1))

    def give_far_partner(st, piece):
        take(st, piece, 4, place(1, 1))
        give(st, piece, 6, place(1, 1), place(0, 3))

    def take_rest(st, piece):
        take(st, piece, 2, place(0, 1))
        take(st, piece, 3, place(1, 3))
        take(st, piece, 5, place(0, 2))
        take(st, piece, 6, place(1, 2))


    into = [
        pltpu.make_async_copy(lesser, x.at[0, pl.ds(0, 2)], s_in.at[1]),
        pltpu.make_async_copy(greater, x.at[0, pl.ds(2, 2)], s_in.at[2]),
    ]
    for copy in into:
        copy.start()
    barrier = pltpu.get_barrier_semaphore()
    for i in range(1, N):
        pl.semaphore_signal(barrier, inc=1, device_id=at((z + i) % N, q, b), device_id_type=MESH)
        pl.semaphore_signal(barrier, inc=1, device_id=at(z, q, (b + i) % N), device_id_type=MESH)
    for i in range(1, Q):
        pl.semaphore_signal(barrier, inc=1, device_id=at(z, (q + i) % Q, b), device_id_type=MESH)
    for i in range(N):
        bb = (b + i) % N

        @pl.when(jnp.logical_and(bb != z, b != z))
        def _():
            pl.semaphore_signal(barrier, inc=1, device_id=at(bb, q, z), device_id_type=MESH)
            if i > 0:
                pl.semaphore_signal(barrier, inc=1, device_id=at(b, q, bb), device_id_type=MESH)

    row = lax.broadcasted_iota(jnp.int32, (ORB + cols, cols), 0) - ORB
    col = lax.broadcasted_iota(jnp.int32, (ORB + cols, cols), 1)
    when = jnp.where(row < 0, Q * J, ((row >> 5) & 3) * J + (row >> 7))
    pre[...] = jnp.where(jnp.logical_and((row & 31) == (col & 31), (col >> 5) < when), 1.0, 0.0).astype(BF16)
    one_hot = (
        lax.broadcasted_iota(jnp.int32, (J * ORB, cols), 1)
        == lax.broadcasted_iota(jnp.int32, (J * ORB, cols), 0) + J * ORB * q
    ).astype(F32).astype(BF16)
    for copy in into:
        copy.wait()
    hb[0, z] = x[0]

    greeted = 2 * (N - 1) + Q - 1

    @pl.when(b == z)
    def _():
        pl.semaphore_wait(barrier, greeted)

    @pl.when(b != z)
    def _():
        pl.semaphore_wait(barrier, greeted + 2 * N - 3)

    for j in range(J):
        mirror_out(0, j)
    history(0, 0, 0)
    history(0, 0, 1)
    for j in range(J):
        quad_out(0, j)

    for st in range(STEPS):
        mirror_on(st, 0)
        if st == 0:
            history(st, 0, 2)
        mirror_on(st, 1)
        mirror_on(st, 2)
        history(st, 1, 0)
        for j in range(J):
            quad_on(st, j)
        history(st, 1, 1)
        for j in range(J):
            quad_in(st, j)
        base = [dot(one_hot, xq[st, c].reshape(cols, cols), NT) for c in range(4)]

        for j in range(J):
            mirror_in(st, j)
            part = slice(j * ORB, (j + 1) * ORB)
            mir = f[st, j].reshape(4, ORB, cols).astype(F32)
            weight = w[part, :]

            def energy(br, bi, mr, mi):
                sr = br * br - bi * bi
                si = 2.0 * br * bi
                return [((sr * mr - si * mi) * weight).astype(BF16), ((sr * mi + si * mr) * weight).astype(BF16)]

            sigma = jnp.concatenate(
                energy(base[2][part], base[3][part], mir[0], mir[1])
                + energy(base[0][part], base[1][part], mir[2], mir[3]),
                axis=0,
            )
            summed = dot(pre[...], sigma, NT).astype(BF16)
            sg[st, j, pl.ds(ORB, cols), pl.ds(pl.multiple_of(wide * b, wide), wide)] = summed[ORB:]
            zs_s[st, :, j * wide:(j + 1) * wide] = summed[:ORB]
            for piece, (k, _, _) in enumerate(PIECES):
                if k == j:
                    give_own(st, piece)

        for i in range(1, N):
            push_if(
                z + i < N, zs_s.at[st], zs_r.at[st, z], s_zs.at[st * N + i], r_zs.at[st * N + i], at((z + i) % N, q, b)
            )

        history(st, 1, 2)
        give_partner(st, 0)
        give_far(st, 0)
        history(st, 2, 0)
        give_partner(st, 1)
        give_far(st, 1)
        history(st, 2, 1)

        carry = jnp.zeros((ORB, cols), F32)
        for i in range(1, N):
            @pl.when(z - i >= 0)
            def _():
                arrive(zs_r.at[st, (z + N - i) % N], r_zs.at[st * N + i])
        for zz in range(N - 1):
            carry = carry + jnp.where(zz < z, zs_r[st, zz].astype(F32), 0.0)
        cs[st, b] = carry.astype(BF16)
        for i in range(1, N):
            k = st * N + i
            push(cs.at[st, b], cs.at[st, b], s_cs.at[k], r_cs.at[k], at(z, q, (b + i) % N))

        give_far_partner(st, 0)
        history(st, 2, 2)
        for piece in (2, 3, 4):
            give_partner(st, piece)
            give_far(st, piece)
        history(st, 3, 0)
        give_far_partner(st, 1)
        history(st, 3, 1)
        history(st, 3, 2)
        for piece in (2, 3, 4):
            give_far_partner(st, piece)
        for j in range(J):
            history(st, 4, j)

        def build(zz, before):
            got = hb[st, zz]
            for j in range(J):
                lr, li, gr, gi = got[0, j], got[1, j], got[2, j], got[3, j]
                rows = pl.ds(pl.multiple_of(wide * zz, wide), wide)
                bm[j, rows, 0:cols] = jnp.concatenate([lr, -li, -gr, gi], axis=0)
                bm[j, rows, cols:2 * cols] = jnp.concatenate([li, lr, -gi, -gr], axis=0)
            total = jnp.sum(got.astype(F32), axis=1)
            return before + jnp.where(zz < z, total, 0.0)

        before = lax.fori_loop(0, N, build, jnp.zeros((4, ORB, cols), F32))
        ax_s[st] = before.astype(BF16)
        for i in range(1, Q):
            k = st * Q + i
            push(ax_s.at[st], ax_r.at[st, q], s_ax.at[k], r_ax.at[k], at(z, (q + i) % Q, b))
        if st == 0:
            @pl.when(q == 0)
            def _():
                ed[...] = hb[0, 0, :, 0]

            for i in range(1, Q):
                push_if(q == 0, hb.at[0, 0, :, 0], ed, s_ed.at[i], r_ed.at[0], at(z, i, b))

        for qq in range(Q - 1):
            total = jnp.sum(xq[st, :, qq].astype(F32), axis=1)
            before = before + jnp.where(qq < q, total, 0.0)
        for i in range(1, Q):
            arrive(ax_r.at[st, (q + Q - i) % Q], r_ax.at[st * Q + i])
            before = before + ax_r[st, (q + Q - i) % Q].astype(F32)
        for c in range(4):
            level = before[c]
            levels = [level]
            for j in range(J - 1):
                level = level + x[st, c, j].astype(F32)
                levels.append(level)
            level = jnp.concatenate(levels, axis=0)
            high = level.astype(BF16)
            low = (level - high.astype(F32)).astype(BF16)
            hop[c] = dot(h3[...], high) + dot(h3[...], low)

        for i in range(1, N):
            arrive(cs.at[st, (b + N - i) % N], r_cs.at[st * N + i])
        for bb in range(N):
            for j in range(J):
                sg[st, j, 0:ORB, bb * wide:(bb + 1) * wide] = cs[st, bb, :, j * wide:(j + 1) * wide]
        take_rest(st, 0)
        acc[...] = dot(sg[st, 0], bm[0])
        take_rest(st, 1)
        acc[...] += dot(sg[st, 1], bm[1])
        lead = None
        for m in range(J):
            take_rest(st, 2 + m)
            lo, hi = (0 if m == 0 else ORB + m * wide), ORB + (m + 1) * wide
            part = acc[lo:hi, :] + dot(sg[st, 2, lo:hi, :], bm[2])
            if m == 0:
                lead = jnp.concatenate([part[:ORB]] * Q, axis=0)
                part = part[ORB:]
            part = part + lead
            acc[ORB + m * wide:hi, :] = part
            rs_s[st, m] = part.reshape(Q, ORB, 2 * cols).astype(BF16)
            for i in range(1, Q):
                to = (q + i) % Q
                k = (st * J + m) * Q + i
                push(rs_s.at[st, m, to], rs_r.at[st, m, q], s_rs.at[k], r_rs.at[k], at(z, to, b))

        if st == 0:
            @pl.when(q != 0)
            def _():
                arrive(ed, r_ed.at[0])

        for m in range(J):
            coll = acc[pl.ds(pl.multiple_of(ORB + m * wide + ORB * q, ORB), ORB), :]
            for i in range(1, Q):
                arrive(rs_r.at[st, m, (q + Q - i) % Q], r_rs.at[(st * J + m) * Q + i])
                coll = coll + rs_r[st, m, (q + Q - i) % Q].astype(F32)
            coll = dt * coll
            for c in range(4):
                edge = ed[c].astype(F32)
                if c % 2 == 0:
                    new = edge + dt * (hop[c + 1, m * ORB:(m + 1) * ORB] + coll[:, cols:])
                else:
                    new = edge - dt * (hop[c - 1, m * ORB:(m + 1) * ORB] + coll[:, :cols])
                new = new.astype(BF16)
                if st + 1 < STEPS:
                    x[st + 1, c, m] = new
                elif c < 2:
                    out_l[c, m] = new
                else:
                    out_g[c - 2, m] = new
            if st + 1 < STEPS:
                hb[st + 1, z, :, m] = x[st + 1, :, m]
                mirror_out(st + 1, m)
                quad_out(st + 1, m)
                history(st + 1, 0, m)

    for drain in drains:
        drain()


def per_device(lesser, greater, hopping, coupling):
    rows, cols = lesser.shape[1:]
    dt = 3.0 / (rows * N * Q // ORB)
    w = jnp.tile(coupling, rows // ORB)[:, None] * jnp.tile(coupling, cols // ORB)[None, :]
    h3 = jnp.kron(jnp.eye(rows // ORB, dtype=hopping.dtype), hopping)
    part = (2, J, ORB, cols)
    wide = 4 * ORB

    def dma(n):
        return pltpu.SemaphoreType.DMA((n,))

    one = [dma(3)]
    pairs = [STEPS * J * N, STEPS * J * N, STEPS * J * 3, STEPS * J * 8, STEPS * len(PIECES) * 7]
    pairs += [STEPS * N, STEPS * N, STEPS * J * Q, STEPS * Q, Q]
    for n in pairs:
        one += [dma(n), dma(n)]
    outs = pl.pallas_call(
        functools.partial(kernel, dt),
        out_shape=[jax.ShapeDtypeStruct(part, BF16)] * 2,
        in_specs=[pl.BlockSpec(memory_space=pl.ANY)] * 2 + [pl.BlockSpec(memory_space=pltpu.VMEM)] * 2,
        out_specs=[pl.BlockSpec(memory_space=pltpu.VMEM)] * 2,
        scratch_shapes=[
            pltpu.VMEM((STEPS, 4, J, ORB, cols), BF16),
            pltpu.VMEM((STEPS, 4, Q, J, ORB, cols), BF16),
            pltpu.VMEM((STEPS, J, N, HALF, cols), BF16),
            pltpu.VMEM((STEPS, J, N, HALF, cols), BF16),
            pltpu.VMEM((STEPS, J, ORB + cols, N * wide), BF16),
            pltpu.VMEM((STEPS, N, 4, J, ORB, cols), BF16),
            pltpu.VMEM((J, N * wide, 2 * cols), BF16),
            pltpu.VMEM((ORB + cols, 2 * cols), F32),
            pltpu.VMEM((ORB + cols, cols), BF16),
            pltpu.VMEM((4, J * ORB, cols), F32),
            pltpu.VMEM((STEPS, ORB, cols), BF16),
            pltpu.VMEM((STEPS, N, ORB, cols), BF16),
            pltpu.VMEM((STEPS, N, ORB, cols), BF16),
            pltpu.VMEM((STEPS, J, Q, ORB, 2 * cols), BF16),
            pltpu.VMEM((STEPS, J, Q, ORB, 2 * cols), BF16),
            pltpu.VMEM((STEPS, 4, ORB, cols), BF16),
            pltpu.VMEM((STEPS, Q, 4, ORB, cols), BF16),
            pltpu.VMEM((4, ORB, cols), BF16),
        ] + one,
        compiler_params=pltpu.CompilerParams(
            collective_id=0, has_side_effects=True, vmem_limit_bytes=56 * 1024 * 1024
        ),
        cost_estimate=pl.CostEstimate(flops=4 * 10**9, bytes_accessed=10**6, transcendentals=0),
    )(lesser.reshape(part), greater.reshape(part), w, h3)
    return outs[0].reshape(lesser.shape), outs[1].reshape(greater.shape)


def solution(mesh):
    in_specs = (P(None, "trow", "tcol"), P(None, "trow", "tcol"), P(), P())
    out_specs = (P(None, "trow", "tcol"), P(None, "trow", "tcol"))
    return jax.shard_map(per_device, mesh=mesh, in_specs=in_specs, out_specs=out_specs, check_vma=False)
```

```python
import functools

import jax
import jax.numpy as jnp
from jax import lax
from jax.experimental import pallas as pl
from jax.experimental.pallas import tpu as pltpu
from jax.sharding import PartitionSpec as P

MESH = pl.DeviceIdType.MESH
ORB = 32
STEPS = 2
N = 8
Q = 4
Y = 4
J = 3
HALF = ORB // 2
F32 = jnp.float32
BF16 = jnp.bfloat16
NT = (((1,), (1,)), ((), ()))
NN = (((1,), (0,)), ((), ()))
PIECES = ((0, 0, Q * J), (1, 0, Q * J), (2, 0, Q), (2, Q, Q), (2, 2 * Q, Q))


def dot(a, b, dims=NN):
    return lax.dot_general(a, b, dims, preferred_element_type=F32)


def kernel(
    dt, lesser, greater, hopping, coupling, out,
    x, xt, xq, t1, f, sg, hb, bm, acc, pre, eye, gather, w, hm, cv, before, hop, zs_s, zs_r, cs, rs_s, rs_r, ax_s, ax_r, ed,
    s_in, s_t1, r_t1, s_t2, r_t2, s_q, r_q, s_h, r_h, s_g, r_g,
    s_zs, r_zs, s_cs, r_cs, s_rs, r_rs, s_ax, r_ax, s_ed, r_ed,
):
    cols = x.shape[-1]
    wide = 4 * ORB
    r = lax.axis_index("trow")
    b = lax.axis_index("tcol")
    z, q = r // Q, r % Q
    xh, y = b // Y, b % Y

    def at(zz, qq, bb):
        return {"trow": zz * Q + qq, "tcol": bb}

    drains = []

    def drain_now(upto):
        for drain in upto:
            drain()

    def copy_of(src, dst, ss, rs, where):
        return pltpu.make_async_remote_copy(
            src_ref=src, dst_ref=dst, send_sem=ss, recv_sem=rs, device_id=where, device_id_type=MESH
        )

    def push(src, dst, ss, rs, where):
        copy = copy_of(src, dst, ss, rs, where)
        copy.start()
        drains.append(copy.wait_send)

    def push_if(cond, src, dst, ss, rs, where):
        @pl.when(cond)
        def _():
            copy_of(src, dst, ss, rs, where).start()

        def drain():
            @pl.when(cond)
            def _():
                copy_of(src, dst, ss, rs, where).wait_send()

        drains.append(drain)

    def arrive(dst, rs):
        copy_of(dst, dst, s_in.at[0], rs, at(z, q, b)).wait_recv()

    def place(dx, dy):
        return ((xh + dx) % 2) * Y + (y + dy) % Y

    up, down = at((z + 1) % N, q, b), at((z + N - 1) % N, q, b)


    def mirror_out(st, j):
        for i in range(1, N):
            p = (b + i) % N
            k = (st * J + j) * N + i
            src = x.at[st, p // 2, j, pl.ds(pl.multiple_of(HALF * (p % 2), HALF), HALF)]
            push(src, t1.at[st, j, b], s_t1.at[k], r_t1.at[k], at(z, q, p))
        t1[st, j, b] = x[st, b // 2, j, pl.ds(pl.multiple_of(HALF * (b % 2), HALF), HALF)]

    def mirror_on(st, j):
        base = (st * J + j) * N
        for i in range(N):
            bb = (b + N - i) % N
            if i > 0:
                arrive(t1.at[st, j, bb], r_t1.at[base + i])
            here = jnp.logical_and(bb == z, b == z)
            push_if(
                jnp.logical_not(here), t1.at[st, j, bb], f.at[st, j, b], s_t2.at[base + i], r_t2.at[base + b], at(bb, q, z)
            )

            @pl.when(here)
            def _():
                f[st, j, b] = t1[st, j, bb]

    def mirror_in(st, j):
        base = (st * J + j) * N
        for i in range(N):
            p = (b + i) % N
            if i > 0:
                arrive(f.at[st, j, p], r_t2.at[base + p])
            else:
                @pl.when(b != z)
                def _():
                    arrive(f.at[st, j, p], r_t2.at[base + p])

    def quad_out(st):
        for c in range(4):
            xt[st, :, c, :, 0:J * ORB] = dot(eye[...], x[st, c].reshape(J * ORB, cols), NT).astype(BF16).reshape(Q, J * ORB, J * ORB)
        lanes = pl.ds(pl.multiple_of(wide * q, wide), wide)
        for i in range(1, Q):
            k = st * Q + i
            to = (q + i) % Q
            push(xt.at[st, to], xq.at[st, :, :, lanes], s_q.at[k], r_q.at[k], at(z, to, b))
        xq[st, :, :, lanes] = xt[st, q]

    def quad_in(st):
        for i in range(1, Q):
            lanes = pl.ds(pl.multiple_of(wide * ((q + Q - i) % Q), wide), wide)
            arrive(xq.at[st, :, :, lanes], r_q.at[st * Q + i])

    def history(st, s, j):
        base = (st * J + j) * 8
        lo, hi = (z + N - s) % N, (z + s) % N
        first, second = (pl.ds(0, 2), pl.ds(2, 2)) if s >= 3 else (pl.ds(0, 4), pl.ds(0, 4))
        if s > 0:
            got = (pl.ds(0, 2), pl.ds(2, 2)) if s == 4 else (pl.ds(0, 4), pl.ds(0, 4))
            arrive(hb.at[st, lo, got[0], j], r_h.at[base + 2 * s - 2])
            arrive(hb.at[st, hi, got[1], j], r_h.at[base + 2 * s - 1])
        if s < 4:
            one, two = hb.at[st, lo, first, j], hb.at[st, hi, second, j]
            from_one, from_two = (x.at[st, :, j], x.at[st, :, j]) if s == 0 else (one, two)
            push(from_one, one, s_h.at[base + 2 * s], r_h.at[base + 2 * s], up)
            push(from_two, two, s_h.at[base + 2 * s + 1], r_h.at[base + 2 * s + 1], down)

    def tile(st, piece, bb):
        k, m, n = PIECES[piece]
        return sg.at[st, k, pl.ds(ORB * (1 + m), ORB * n), pl.ds(pl.multiple_of(wide * bb, wide), wide)]

    def give(st, piece, way, bb, to):
        k = (st * len(PIECES) + piece) * 7 + way
        push(tile(st, piece, bb), tile(st, piece, bb), s_g.at[k], r_g.at[k], at(z, q, to))

    def take(st, piece, way, bb):
        arrive(tile(st, piece, bb), r_g.at[(st * len(PIECES) + piece) * 7 + way])

    def give_own(st, piece):
        give(st, piece, 0, b, place(1, 0))
        give(st, piece, 1, b, place(0, 1))
        give(st, piece, 2, b, place(0, 3))

    def give_partner(st, piece):
        take(st, piece, 0, place(1, 0))
        give(st, piece, 3, place(1, 0), place(0, 1))
        give(st, piece, 4, place(1, 0), place(0, 3))

    def give_far(st, piece):
        take(st, piece, 1, place(0, 3))
        give(st, piece, 5, place(0, 3), place(0, 1))

    def give_far_partner(st, piece):
        take(st, piece, 4, place(1, 1))
        give(st, piece, 6, place(1, 1), place(0, 3))

    def take_rest(st, piece):
        take(st, piece, 2, place(0, 1))
        take(st, piece, 3, place(1, 3))
        take(st, piece, 5, place(0, 2))
        take(st, piece, 6, place(1, 2))


    into = [
        pltpu.make_async_copy(lesser, x.at[0, pl.ds(0, 2)], s_in.at[1]),
        pltpu.make_async_copy(greater, x.at[0, pl.ds(2, 2)], s_in.at[2]),
        pltpu.make_async_copy(hopping, hm, s_in.at[3]),
        pltpu.make_async_copy(coupling, cv, s_in.at[4]),
    ]
    for copy in into:
        copy.start()
    barrier = pltpu.get_barrier_semaphore()
    for i in range(1, N):
        pl.semaphore_signal(barrier, inc=1, device_id=at((z + i) % N, q, b), device_id_type=MESH)
        pl.semaphore_signal(barrier, inc=1, device_id=at(z, q, (b + i) % N), device_id_type=MESH)
    for i in range(1, Q):
        pl.semaphore_signal(barrier, inc=1, device_id=at(z, (q + i) % Q, b), device_id_type=MESH)
    for i in range(N):
        bb = (b + i) % N

        @pl.when(jnp.logical_and(bb != z, b != z))
        def _():
            pl.semaphore_signal(barrier, inc=1, device_id=at(bb, q, z), device_id_type=MESH)
            if i > 0:
                pl.semaphore_signal(barrier, inc=1, device_id=at(b, q, bb), device_id_type=MESH)

    row = lax.broadcasted_iota(jnp.int32, (ORB + cols, cols), 0) - ORB
    col = lax.broadcasted_iota(jnp.int32, (ORB + cols, cols), 1)
    when = jnp.where(row < 0, Q * J, ((row >> 5) & 3) * J + (row >> 7))
    pre[...] = jnp.where(jnp.logical_and((row & 31) == (col & 31), (col >> 5) < when), 1.0, 0.0).astype(BF16)
    eye[...] = jnp.where(
        lax.broadcasted_iota(jnp.int32, (cols, cols), 0) == lax.broadcasted_iota(jnp.int32, (cols, cols), 1), 1.0, 0.0
    ).astype(BF16)
    from_q = lax.broadcasted_iota(jnp.int32, (Q * wide, cols), 0)
    to_q = lax.broadcasted_iota(jnp.int32, (Q * wide, cols), 1)
    packed = (from_q >> 7) * (J * ORB) + (from_q & 127)
    gather[...] = jnp.where(jnp.logical_and((from_q & 127) < J * ORB, packed == to_q), 1.0, 0.0).astype(BF16)
    xt[...] = jnp.zeros_like(xt)
    for copy in into:
        copy.wait()
    across = jnp.broadcast_to(cv[...], (ORB, ORB))
    same = lax.broadcasted_iota(jnp.int32, (ORB, ORB), 0) == lax.broadcasted_iota(jnp.int32, (ORB, ORB), 1)
    tall = jnp.sum(jnp.where(same, across, 0.0), axis=1, keepdims=True)
    same = lax.broadcasted_iota(jnp.int32, (ORB, cols), 0) == (lax.broadcasted_iota(jnp.int32, (ORB, cols), 1) & 31)
    flat = jnp.sum(jnp.where(same, jnp.broadcast_to(tall, (ORB, cols)), 0.0), axis=0, keepdims=True)
    w[...] = tall * flat
    hb[0, z] = x[0]

    greeted = 2 * (N - 1) + Q - 1

    @pl.when(b == z)
    def _():
        pl.semaphore_wait(barrier, greeted)

    @pl.when(b != z)
    def _():
        pl.semaphore_wait(barrier, greeted + 2 * N - 3)

    def build(st, zz):
        got = hb[st, zz]
        rows = pl.ds(pl.multiple_of(wide * zz, wide), wide)
        for j in range(J):
            lr, li, gr, gi = got[0, j], got[1, j], got[2, j], got[3, j]
            bm[j, rows, 0:cols] = jnp.concatenate([lr, -li, -gr, gi], axis=0)
            bm[j, rows, cols:2 * cols] = jnp.concatenate([li, lr, -gi, -gr], axis=0)
        before[...] += jnp.where(zz < z, jnp.sum(got.astype(F32), axis=1), 0.0)

    mirror_out(0, 0)
    history(0, 0, 0)
    history(0, 0, 1)
    quad_out(0)
    mirror_out(0, 1)
    mirror_out(0, 2)

    for st in range(STEPS):
        earlier, drains[:] = list(drains), []
        before[...] = jnp.zeros_like(before)
        mirror_on(st, 0)
        if st == 0:
            history(st, 0, 2)
        mirror_on(st, 1)
        mirror_on(st, 2)
        history(st, 1, 0)
        history(st, 1, 1)
        quad_in(st)
        base = [dot(xq[st, c], gather[...]) for c in range(4)]

        for j in range(J):
            mirror_in(st, j)
            part = slice(j * ORB, (j + 1) * ORB)
            mir = f[st, j].reshape(4, ORB, cols).astype(F32)
            weight = w[...]

            def energy(br, bi, mr, mi):
                sr = br * br - bi * bi
                si = 2.0 * br * bi
                return [((sr * mr - si * mi) * weight).astype(BF16), ((sr * mi + si * mr) * weight).astype(BF16)]

            sigma = jnp.concatenate(
                energy(base[2][part], base[3][part], mir[0], mir[1])
                + energy(base[0][part], base[1][part], mir[2], mir[3]),
                axis=0,
            )
            summed = dot(pre[...], sigma, NT).astype(BF16)
            sg[st, j, pl.ds(ORB, cols), pl.ds(pl.multiple_of(wide * b, wide), wide)] = summed[ORB:]
            zs_s[st, :, j * wide:(j + 1) * wide] = summed[:ORB]
            for piece, (k, _, _) in enumerate(PIECES):
                if k == j:
                    give_own(st, piece)

        for i in range(1, N):
            push_if(
                z + i < N, zs_s.at[st], zs_r.at[st, z], s_zs.at[st * N + i], r_zs.at[st * N + i], at((z + i) % N, q, b)
            )

        earlier, drains[:] = earlier + drains, []
        history(st, 1, 2)
        build(st, z)
        give_partner(st, 0)
        give_far(st, 0)
        history(st, 2, 0)
        build(st, (z + 1) % N)
        build(st, (z + N - 1) % N)
        give_partner(st, 1)
        give_far(st, 1)
        history(st, 2, 1)

        carry = jnp.zeros((ORB, cols), F32)
        for i in range(1, N):
            @pl.when(z - i >= 0)
            def _():
                arrive(zs_r.at[st, (z + N - i) % N], r_zs.at[st * N + i])
        for zz in range(N - 1):
            carry = carry + jnp.where(zz < z, zs_r[st, zz].astype(F32), 0.0)
        cs[st, b] = carry.astype(BF16)
        for i in range(1, N):
            k = st * N + i
            push(cs.at[st, b], cs.at[st, b], s_cs.at[k], r_cs.at[k], at(z, q, (b + i) % N))

        give_far_partner(st, 0)
        history(st, 2, 2)
        for piece in (2, 3, 4):
            give_partner(st, piece)
            give_far(st, piece)
        build(st, (z + 2) % N)
        build(st, (z + N - 2) % N)
        history(st, 3, 0)
        give_far_partner(st, 1)
        history(st, 3, 1)
        history(st, 3, 2)
        for piece in (2, 3, 4):
            give_far_partner(st, piece)
        build(st, (z + 3) % N)
        build(st, (z + N - 3) % N)
        drain_now(earlier)
        for j in range(J):
            history(st, 4, j)
        build(st, (z + 4) % N)

        ax_s[st, 0] = before[...].astype(BF16)
        ax_s[st, 1] = (before[...] + jnp.sum(x[st].astype(F32), axis=1)).astype(BF16)
        for i in range(1, Q):
            k = st * Q + i
            to = (q + i) % Q
            push(ax_s.at[st, jnp.where(to > q, 1, 0)], ax_r.at[st, q], s_ax.at[k], r_ax.at[k], at(z, to, b))
        if st == 0:
            @pl.when(q == 0)
            def _():
                ed[...] = hb[0, 0, :, 0]

            for i in range(1, Q):
                push_if(q == 0, hb.at[0, 0, :, 0], ed, s_ed.at[i], r_ed.at[0], at(z, i, b))

        for i in range(1, N):
            arrive(cs.at[st, (b + N - i) % N], r_cs.at[st * N + i])
        for bb in range(N):
            for j in range(J):
                sg[st, j, 0:ORB, bb * wide:(bb + 1) * wide] = cs[st, bb, :, j * wide:(j + 1) * wide]
        take_rest(st, 0)
        acc[...] = dot(sg[st, 0], bm[0])
        take_rest(st, 1)
        acc[...] += dot(sg[st, 1], bm[1])
        lead = None
        for m in range(J):
            take_rest(st, 2 + m)
            lo, hi = (0 if m == 0 else ORB + m * wide), ORB + (m + 1) * wide
            part = acc[lo:hi, :] + dot(sg[st, 2, lo:hi, :], bm[2])
            if m == 0:
                lead = jnp.concatenate([part[:ORB]] * Q, axis=0)
                part = part[ORB:]
            part = part + lead
            acc[ORB + m * wide:hi, :] = part
            rs_s[st, m] = part.reshape(Q, ORB, 2 * cols).astype(BF16)
            for i in range(1, Q):
                to = (q + i) % Q
                k = (st * J + m) * Q + i
                push(rs_s.at[st, m, to], rs_r.at[st, m, q], s_rs.at[k], r_rs.at[k], at(z, to, b))

        level = before[...]
        for i in range(1, Q):
            arrive(ax_r.at[st, (q + Q - i) % Q], r_ax.at[st * Q + i])
            level = level + ax_r[st, (q + Q - i) % Q].astype(F32)
        for c in range(4):
            run = level[c]
            runs = [run]
            for j in range(J - 1):
                run = run + x[st, c, j].astype(F32)
                runs.append(run)
            run = jnp.concatenate(runs, axis=1)
            high = run.astype(BF16)
            low = (run - high.astype(F32)).astype(BF16)
            hop[c] = dot(hm[...], high) + dot(hm[...], low)
        if st == 0:
            @pl.when(q != 0)
            def _():
                arrive(ed, r_ed.at[0])
        earlier, drains[:] = list(drains), []
        drain_now(earlier)

        for m in range(J):
            coll = acc[pl.ds(pl.multiple_of(ORB + m * wide + ORB * q, ORB), ORB), :]
            for i in range(1, Q):
                arrive(rs_r.at[st, m, (q + Q - i) % Q], r_rs.at[(st * J + m) * Q + i])
                coll = coll + rs_r[st, m, (q + Q - i) % Q].astype(F32)
            coll = dt * coll
            for c in range(4):
                edge = ed[c].astype(F32)
                lanes = slice(m * cols, (m + 1) * cols)
                if c % 2 == 0:
                    new = edge + dt * (hop[c + 1, :, lanes] + coll[:, cols:])
                else:
                    new = edge - dt * (hop[c - 1, :, lanes] + coll[:, :cols])
                if st + 1 < STEPS:
                    x[st + 1, c, m] = new.astype(BF16)
                else:
                    out[c, m] = new.astype(BF16)
            if st + 1 < STEPS:
                hb[st + 1, z, :, m] = x[st + 1, :, m]
                mirror_out(st + 1, m)
                history(st + 1, 0, m)
        if st + 1 < STEPS:
            quad_out(st + 1)

    drain_now(drains)


def per_device(lesser, greater, hopping, coupling):
    rows, cols = lesser.shape[1:]
    dt = 3.0 / (rows * N * Q // ORB)
    wide = 4 * ORB

    def dma(n):
        return pltpu.SemaphoreType.DMA((n,))

    sems = [dma(5)]
    pairs = [STEPS * J * N, STEPS * J * N, STEPS * Q, STEPS * J * 8, STEPS * len(PIECES) * 7]
    pairs += [STEPS * N, STEPS * N, STEPS * J * Q, STEPS * Q, Q]
    for n in pairs:
        sems += [dma(n), dma(n)]
    buffers = [
        ((STEPS, 4, J, ORB, cols), BF16),
        ((STEPS, Q, 4, J * ORB, wide), BF16),
        ((STEPS, 4, J * ORB, Q * wide), BF16),
        ((STEPS, J, N, HALF, cols), BF16),
        ((STEPS, J, N, HALF, cols), BF16),
        ((STEPS, J, ORB + cols, N * wide), BF16),
        ((STEPS, N, 4, J, ORB, cols), BF16),
        ((J, N * wide, 2 * cols), BF16),
        ((ORB + cols, 2 * cols), F32),
        ((ORB + cols, cols), BF16),
        ((cols, cols), BF16),
        ((Q * wide, cols), BF16),
        ((ORB, cols), F32),
        ((ORB, ORB), BF16),
        ((1, ORB), F32),
        ((4, ORB, cols), F32),
        ((4, ORB, J * cols), F32),
        ((STEPS, ORB, cols), BF16),
        ((STEPS, N, ORB, cols), BF16),
        ((STEPS, N, ORB, cols), BF16),
        ((STEPS, J, Q, ORB, 2 * cols), BF16),
        ((STEPS, J, Q, ORB, 2 * cols), BF16),
        ((STEPS, 2, 4, ORB, cols), BF16),
        ((STEPS, Q, 4, ORB, cols), BF16),
        ((4, ORB, cols), BF16),
    ]
    part = (2, J, ORB, cols)
    new = pl.pallas_call(
        functools.partial(kernel, dt),
        out_shape=jax.ShapeDtypeStruct((4, J, ORB, cols), BF16),
        in_specs=[pl.BlockSpec(memory_space=pl.ANY)] * 4,
        out_specs=pl.BlockSpec(memory_space=pltpu.VMEM),
        scratch_shapes=[pltpu.VMEM(shape, dtype) for shape, dtype in buffers] + sems,
        compiler_params=pltpu.CompilerParams(
            collective_id=0, has_side_effects=True, vmem_limit_bytes=56 * 1024 * 1024
        ),
        cost_estimate=pl.CostEstimate(flops=4 * 10**9, bytes_accessed=10**6, transcendentals=0),
    )(lesser.reshape(part), greater.reshape(part), hopping, coupling.reshape(1, ORB))
    new = new.reshape(4, rows, cols)
    return new[:2], new[2:]


def solution(mesh):
    in_specs = (P(None, "trow", "tcol"), P(None, "trow", "tcol"), P(), P())
    out_specs = (P(None, "trow", "tcol"), P(None, "trow", "tcol"))
    return jax.shard_map(per_device, mesh=mesh, in_specs=in_specs, out_specs=out_specs, check_vma=False)
```

```python
import functools

import jax
import jax.numpy as jnp
from jax import lax
from jax.experimental import pallas as pl
from jax.experimental.pallas import tpu as pltpu
from jax.sharding import PartitionSpec as P

MESH = pl.DeviceIdType.MESH
ORB = 32
STEPS = 2
N = 8
Q = 4
Y = 4
J = 3
HALF = ORB // 2
F32 = jnp.float32
BF16 = jnp.bfloat16
NT = (((1,), (1,)), ((), ()))
NN = (((1,), (0,)), ((), ()))
PIECES = ((0, 0, Q * J), (1, 0, Q * J), (2, 0, Q), (2, Q, Q), (2, 2 * Q, Q))


def dot(a, b, dims=NN):
    return lax.dot_general(a, b, dims, preferred_element_type=F32)


def kernel(
    dt, lesser, greater, hopping, coupling, out,
    x, xt, xq, t1, f, sg, hb, bm, acc, pre, eye, gather, w, hm, cv, before, hop, zs_s, zs_r, cs, rs_s, rs_r, ax_s, ax_r, ed,
    s_in, s_t1, r_t1, s_t2, r_t2, s_q, r_q, s_h, r_h, s_g, r_g,
    s_zs, r_zs, s_cs, r_cs, s_rs, r_rs, s_ax, r_ax, s_ed, r_ed,
):
    cols = x.shape[-1]
    wide = 4 * ORB
    r = lax.axis_index("trow")
    b = lax.axis_index("tcol")
    z, q = r // Q, r % Q
    xh, y = b // Y, b % Y

    def at(zz, qq, bb):
        return {"trow": zz * Q + qq, "tcol": bb}

    drains = []

    def drain_now(upto):
        for drain in upto:
            drain()

    def copy_of(src, dst, ss, rs, where):
        return pltpu.make_async_remote_copy(
            src_ref=src, dst_ref=dst, send_sem=ss, recv_sem=rs, device_id=where, device_id_type=MESH
        )

    def push(src, dst, ss, rs, where):
        copy_of(src, dst, ss, rs, where).start()

    def owe(ref, ss):
        drains.append(copy_of(ref, ref, ss, s_in.at[0], at(z, q, b)).wait_send)

    def arrive(ref, rs):
        copy_of(ref, ref, s_in.at[0], rs, at(z, q, b)).wait_recv()

    def place(dx, dy):
        return ((xh + dx) % 2) * Y + (y + dy) % Y

    up, down = at((z + 1) % N, q, b), at((z + N - 1) % N, q, b)


    def mirror_out(st, j):
        k = st * J + j
        for i in range(1, N):
            p = (b + i) % N
            src = x.at[st, p // 2, j, pl.ds(pl.multiple_of(HALF * (p % 2), HALF), HALF)]
            push(src, t1.at[st, j, b], s_t1.at[k], r_t1.at[k], at(z, q, p))
        owe(t1.at[st, j, pl.ds(0, N - 1)], s_t1.at[k])
        t1[st, j, b] = x[st, b // 2, j, pl.ds(pl.multiple_of(HALF * (b % 2), HALF), HALF)]

    def mirror_on(st, j):
        k = st * J + j
        arrive(t1.at[st, j, pl.ds(0, N - 1)], r_t1.at[k])
        for i in range(N):
            bb = (b + N - i) % N
            here = jnp.logical_and(bb == z, b == z)

            @pl.when(jnp.logical_not(here))
            def _():
                push(t1.at[st, j, bb], f.at[st, j, b], s_t2.at[k], r_t2.at[k], at(bb, q, z))

            @pl.when(here)
            def _():
                f[st, j, b] = t1[st, j, bb]

        def drain():
            for n, cond in ((N - 1, b == z), (N, b != z)):
                @pl.when(cond)
                def _():
                    ref = t1.at[st, j, pl.ds(0, n)]
                    copy_of(ref, ref, s_t2.at[k], s_in.at[0], at(z, q, b)).wait_send()

        drains.append(drain)

    def mirror_in(st, j):
        for n, cond in ((N - 1, b == z), (N, b != z)):
            @pl.when(cond)
            def _():
                arrive(f.at[st, j, pl.ds(0, n)], r_t2.at[st * J + j])

    def quad_out(st):
        for c in range(4):
            xt[st, :, c, :, 0:J * ORB] = dot(eye[...], x[st, c].reshape(J * ORB, cols), NT).astype(BF16).reshape(Q, J * ORB, J * ORB)
        lanes = pl.ds(pl.multiple_of(wide * q, wide), wide)
        for j in range(J):
            part = pl.ds(j * ORB, ORB)
            k = st * J + j
            for i in range(1, Q):
                to = (q + i) % Q
                push(xt.at[st, to, :, part], xq.at[st, :, part, lanes], s_q.at[k], r_q.at[k], at(z, to, b))
            owe(xq.at[st, :, part, pl.ds(0, (Q - 1) * wide)], s_q.at[k])
        xq[st, :, :, lanes] = xt[st, q]

    def quad_in(st, j):
        arrive(xq.at[st, :, pl.ds(j * ORB, ORB), pl.ds(0, (Q - 1) * wide)], r_q.at[st * J + j])

    def history(st, s, j):
        k = st * J + j
        lo, hi = (z + N - s) % N, (z + s) % N
        if s > 0:
            arrive(hb.at[st, pl.ds(0, 1 if s == 4 else 2), :, j], r_h.at[4 * k + s - 1])
        if s < 4:
            first, second = (pl.ds(0, 2), pl.ds(2, 2)) if s == 3 else (pl.ds(0, 4), pl.ds(0, 4))
            one, two = hb.at[st, lo, first, j], hb.at[st, hi, second, j]
            from_one, from_two = (x.at[st, :, j], x.at[st, :, j]) if s == 0 else (one, two)
            push(from_one, one, s_h.at[k], r_h.at[4 * k + s], up)
            push(from_two, two, s_h.at[k], r_h.at[4 * k + s], down)
        if s == 3:
            owe(hb.at[st, pl.ds(0, N - 1), :, j], s_h.at[k])

    def tile(st, piece, bb):
        k, m, n = PIECES[piece]
        return sg.at[st, k, pl.ds(ORB * (1 + m), ORB * n), pl.ds(pl.multiple_of(wide * bb, wide), wide)]

    WAIT = (0, 1, 3, 3, 2, 3, 3)

    def several(st, piece, n):
        k, m, rows = PIECES[piece]
        return sg.at[st, k, pl.ds(ORB * (1 + m), ORB * rows), pl.ds(0, n * wide)]

    def give(st, piece, way, bb, to):
        k = st * len(PIECES) + piece
        push(tile(st, piece, bb), tile(st, piece, bb), s_g.at[k], r_g.at[4 * k + WAIT[way]], at(z, q, to))

    def take(st, piece, wait):
        arrive(several(st, piece, 4 if wait == 3 else 1), r_g.at[4 * (st * len(PIECES) + piece) + wait])

    def give_own(st, piece):
        give(st, piece, 0, b, place(1, 0))
        give(st, piece, 1, b, place(0, 1))
        give(st, piece, 2, b, place(0, 3))

    def give_partner(st, piece):
        take(st, piece, 0)
        give(st, piece, 3, place(1, 0), place(0, 1))
        give(st, piece, 4, place(1, 0), place(0, 3))

    def give_far(st, piece):
        take(st, piece, 1)
        give(st, piece, 5, place(0, 3), place(0, 1))

    def give_far_partner(st, piece):
        take(st, piece, 2)
        give(st, piece, 6, place(1, 1), place(0, 3))
        owe(several(st, piece, 7), s_g.at[st * len(PIECES) + piece])

    def take_rest(st, piece):
        take(st, piece, 3)


    into = [
        pltpu.make_async_copy(lesser, x.at[0, pl.ds(0, 2)], s_in.at[1]),
        pltpu.make_async_copy(greater, x.at[0, pl.ds(2, 2)], s_in.at[2]),
        pltpu.make_async_copy(hopping, hm, s_in.at[3]),
        pltpu.make_async_copy(coupling, cv, s_in.at[4]),
    ]
    for copy in into:
        copy.start()
    barrier = pltpu.get_barrier_semaphore()
    for i in range(1, N):
        pl.semaphore_signal(barrier, inc=1, device_id=at((z + i) % N, q, b), device_id_type=MESH)
        pl.semaphore_signal(barrier, inc=1, device_id=at(z, q, (b + i) % N), device_id_type=MESH)
    for i in range(1, Q):
        pl.semaphore_signal(barrier, inc=1, device_id=at(z, (q + i) % Q, b), device_id_type=MESH)
    row = lax.broadcasted_iota(jnp.int32, (ORB + cols, cols), 0) - ORB
    col = lax.broadcasted_iota(jnp.int32, (ORB + cols, cols), 1)
    when = jnp.where(row < 0, Q * J, ((row >> 5) & 3) * J + (row >> 7))
    pre[...] = jnp.where(jnp.logical_and((row & 31) == (col & 31), (col >> 5) < when), 1.0, 0.0).astype(BF16)
    eye[...] = jnp.where(
        lax.broadcasted_iota(jnp.int32, (cols, cols), 0) == lax.broadcasted_iota(jnp.int32, (cols, cols), 1), 1.0, 0.0
    ).astype(BF16)
    from_q = lax.broadcasted_iota(jnp.int32, (Q * wide, cols), 0)
    to_q = lax.broadcasted_iota(jnp.int32, (Q * wide, cols), 1)
    packed = (from_q >> 7) * (J * ORB) + (from_q & 127)
    gather[...] = jnp.where(jnp.logical_and((from_q & 127) < J * ORB, packed == to_q), 1.0, 0.0).astype(BF16)
    xt[...] = jnp.zeros_like(xt)
    for copy in into:
        copy.wait()
    across = jnp.broadcast_to(cv[...], (ORB, ORB))
    same = lax.broadcasted_iota(jnp.int32, (ORB, ORB), 0) == lax.broadcasted_iota(jnp.int32, (ORB, ORB), 1)
    tall = jnp.sum(jnp.where(same, across, 0.0), axis=1, keepdims=True)
    same = lax.broadcasted_iota(jnp.int32, (ORB, cols), 0) == (lax.broadcasted_iota(jnp.int32, (ORB, cols), 1) & 31)
    flat = jnp.sum(jnp.where(same, jnp.broadcast_to(tall, (ORB, cols)), 0.0), axis=0, keepdims=True)
    w[...] = tall * flat

    hb[0, z] = x[0]

    pl.semaphore_wait(barrier, 2 * (N - 1) + Q - 1)

    def build(st, zz):
        got = hb[st, zz]
        rows = pl.ds(pl.multiple_of(wide * zz, wide), wide)
        for j in range(J):
            lr, li, gr, gi = got[0, j], got[1, j], got[2, j], got[3, j]
            bm[j, rows, 0:cols] = jnp.concatenate([lr, -li, -gr, gi], axis=0)
            bm[j, rows, cols:2 * cols] = jnp.concatenate([li, lr, -gi, -gr], axis=0)
        before[...] += jnp.where(zz < z, jnp.sum(got.astype(F32), axis=1), 0.0)

    mirror_out(0, 0)
    history(0, 0, 0)
    history(0, 0, 1)

    quad_out(0)
    mirror_out(0, 1)
    mirror_out(0, 2)

    for st in range(STEPS):
        earlier, drains[:] = list(drains), []
        before[...] = jnp.zeros_like(before)
        mirror_on(st, 0)
        if st == 0:
            history(st, 0, 2)
        mirror_on(st, 1)
        mirror_on(st, 2)
        history(st, 1, 0)

        for j in range(J):
            quad_in(st, j)
            base = [dot(xq[st, c, j * ORB:(j + 1) * ORB], gather[...]) for c in range(4)]
            mirror_in(st, j)
            mir = f[st, j].reshape(4, ORB, cols).astype(F32)
            weight = w[...]

            def energy(br, bi, mr, mi):
                sr = br * br - bi * bi
                si = 2.0 * br * bi
                return [((sr * mr - si * mi) * weight).astype(BF16), ((sr * mi + si * mr) * weight).astype(BF16)]

            sigma = jnp.concatenate(
                energy(base[2], base[3], mir[0], mir[1]) + energy(base[0], base[1], mir[2], mir[3]),
                axis=0,
            )
            summed = dot(pre[...], sigma, NT).astype(BF16)
            sg[st, j, pl.ds(ORB, cols), pl.ds(pl.multiple_of(wide * b, wide), wide)] = summed[ORB:]
            zs_s[st, :, j * wide:(j + 1) * wide] = summed[:ORB]
            for piece, (k, _, _) in enumerate(PIECES):
                if k == j:
                    give_own(st, piece)
            if j < 2:
                history(st, 1, 1 + j)

        for i in range(1, N):
            push(zs_s.at[st], zs_r.at[st, z], s_zs.at[st], r_zs.at[st], at((z + i) % N, q, b))
        owe(zs_r.at[st, pl.ds(0, N - 1)], s_zs.at[st])

        earlier, drains[:] = earlier + drains, []
        history(st, 2, 0)
        build(st, z)
        give_partner(st, 0)
        give_far(st, 0)
        history(st, 2, 1)
        build(st, (z + 1) % N)
        build(st, (z + N - 1) % N)
        give_partner(st, 1)
        give_far(st, 1)
        history(st, 2, 2)

        carry = jnp.zeros((ORB, cols), F32)
        arrive(zs_r.at[st, pl.ds(0, N - 1)], r_zs.at[st])
        for zz in range(N - 1):
            carry = carry + jnp.where(zz < z, zs_r[st, zz].astype(F32), 0.0)
        cs[st, b] = carry.astype(BF16)
        for i in range(1, N):
            push(cs.at[st, b], cs.at[st, b], s_cs.at[st], r_cs.at[st], at(z, q, (b + i) % N))
        owe(cs.at[st, pl.ds(0, N - 1)], s_cs.at[st])

        give_far_partner(st, 0)
        history(st, 3, 0)
        give_partner(st, 2)
        give_far(st, 2)
        give_far_partner(st, 1)
        history(st, 3, 1)
        build(st, (z + 2) % N)
        build(st, (z + N - 2) % N)
        for piece in (3, 4):
            give_partner(st, piece)
            give_far(st, piece)
        history(st, 3, 2)
        for piece in (2, 3, 4):
            give_far_partner(st, piece)
        build(st, (z + 3) % N)
        build(st, (z + N - 3) % N)
        drain_now(earlier)
        for j in range(J):
            history(st, 4, j)
        build(st, (z + 4) % N)

        ax_s[st, 0] = before[...].astype(BF16)
        ax_s[st, 1] = (before[...] + jnp.sum(x[st].astype(F32), axis=1)).astype(BF16)
        sib = (q // 2) * 2 + (1 - q % 2)
        par = (q + 2) % Q
        dia = (sib + 2) % Q
        k = st * 3
        push(ax_s.at[st, 1 - q // 2], ax_r.at[st, q], s_ax.at[st], r_ax.at[k], at(z, par, b))
        push(ax_s.at[st, 1 - q % 2], ax_r.at[st, q], s_ax.at[st], r_ax.at[k + 1], at(z, sib, b))
        if st == 0:
            @pl.when(q == 0)
            def _():
                ed[...] = hb[0, 0, :, 0]
                for i in range(1, Q):
                    push(hb.at[0, 0, :, 0], ed, s_ed.at[0], r_ed.at[0], at(z, i, b))

        arrive(cs.at[st, pl.ds(0, N - 1)], r_cs.at[st])
        for bb in range(N):
            for j in range(J):
                sg[st, j, 0:ORB, bb * wide:(bb + 1) * wide] = cs[st, bb, :, j * wide:(j + 1) * wide]
        take_rest(st, 0)
        acc[...] = dot(sg[st, 0], bm[0])
        take_rest(st, 1)
        acc[...] += dot(sg[st, 1], bm[1])

        def rows_of(m, qq):
            return acc[pl.ds(pl.multiple_of(ORB + m * wide + ORB * qq, ORB), ORB), :]

        def cross(m):
            k = 2 * (st * J + m)
            arrive(rs_r.at[st, m, pl.ds(0, 2)], r_rs.at[k])
            rs_s[st, m, 2] = (rows_of(m, par) + rs_r[st, m, 1].astype(F32)).astype(BF16)
            push(rs_s.at[st, m, 2], rs_r.at[st, m, 2], s_rs.at[k + 1], r_rs.at[k + 1], at(z, par, b))
            owe(rs_s.at[st, m, 2], s_rs.at[k + 1])

        lead = None
        for m in range(J):
            take_rest(st, 2 + m)
            lo, hi = (0 if m == 0 else ORB + m * wide), ORB + (m + 1) * wide
            part = acc[lo:hi, :] + dot(sg[st, 2, lo:hi, :], bm[2])
            if m == 0:
                lead = jnp.concatenate([part[:ORB]] * Q, axis=0)
                part = part[ORB:]
            part = part + lead
            acc[ORB + m * wide:hi, :] = part
            rs_s[st, m, 0] = rows_of(m, sib).astype(BF16)
            rs_s[st, m, 1] = rows_of(m, dia).astype(BF16)
            k = 2 * (st * J + m)
            push(rs_s.at[st, m, pl.ds(0, 2)], rs_r.at[st, m, pl.ds(0, 2)], s_rs.at[k], r_rs.at[k], at(z, sib, b))
            owe(rs_s.at[st, m, pl.ds(0, 2)], s_rs.at[k])
            if m > 0:
                cross(m - 1)
        cross(J - 1)

        level = before[...]
        k = st * 3
        arrive(ax_r.at[st, par], r_ax.at[k])
        push(ax_r.at[st, par], ax_r.at[st, par], s_ax.at[st], r_ax.at[k + 2], at(z, sib, b))
        owe(ax_r.at[st, pl.ds(0, 3)], s_ax.at[st])
        arrive(ax_r.at[st, sib], r_ax.at[k + 1])
        arrive(ax_r.at[st, dia], r_ax.at[k + 2])
        for other in (par, sib, dia):
            level = level + ax_r[st, other].astype(F32)
        for c in range(4):
            run = level[c]
            runs = [run]
            for j in range(J - 1):
                run = run + x[st, c, j].astype(F32)
                runs.append(run)
            run = jnp.concatenate(runs, axis=1)
            high = run.astype(BF16)
            low = (run - high.astype(F32)).astype(BF16)
            hop[c] = dot(hm[...], high) + dot(hm[...], low)
        if st == 0:
            @pl.when(q != 0)
            def _():
                arrive(ed, r_ed.at[0])

            def drain():
                @pl.when(q == 0)
                def _():
                    ref = ax_r.at[0, pl.ds(0, 3)]
                    copy_of(ref, ref, s_ed.at[0], s_in.at[0], at(z, q, b)).wait_send()

            drains.append(drain)
        earlier, drains[:] = list(drains), []
        drain_now(earlier)

        for m in range(J):
            arrive(rs_r.at[st, m, 2], r_rs.at[2 * (st * J + m) + 1])
            coll = rows_of(m, q) + rs_r[st, m, 0].astype(F32) + rs_r[st, m, 2].astype(F32)
            coll = dt * coll
            for c in range(4):
                edge = ed[c].astype(F32)
                lanes = slice(m * cols, (m + 1) * cols)
                if c % 2 == 0:
                    new = edge + dt * (hop[c + 1, :, lanes] + coll[:, cols:])
                else:
                    new = edge - dt * (hop[c - 1, :, lanes] + coll[:, :cols])
                if st + 1 < STEPS:
                    x[st + 1, c, m] = new.astype(BF16)
                else:
                    out[c, m] = new.astype(BF16)
            if st + 1 < STEPS:
                hb[st + 1, z, :, m] = x[st + 1, :, m]
                mirror_out(st + 1, m)
                history(st + 1, 0, m)
        if st + 1 < STEPS:
            quad_out(st + 1)

    drain_now(drains)


def per_device(lesser, greater, hopping, coupling):
    rows, cols = lesser.shape[1:]
    dt = 3.0 / (rows * N * Q // ORB)
    wide = 4 * ORB

    def dma(n):
        return pltpu.SemaphoreType.DMA((n,))

    pieces = STEPS * J
    sems = [dma(5)]
    for sent, got in (
        (pieces, pieces), (pieces, pieces), (pieces, pieces), (pieces, 4 * pieces),
        (STEPS * len(PIECES), STEPS * len(PIECES) * 4), (STEPS, STEPS), (STEPS, STEPS),
        (2 * pieces, 2 * pieces), (STEPS, 3 * STEPS), (1, 1),
    ):
        sems += [dma(sent), dma(got)]
    buffers = [
        ((STEPS, 4, J, ORB, cols), BF16),
        ((STEPS, Q, 4, J * ORB, wide), BF16),
        ((STEPS, 4, J * ORB, Q * wide), BF16),
        ((STEPS, J, N, HALF, cols), BF16),
        ((STEPS, J, N, HALF, cols), BF16),
        ((STEPS, J, ORB + cols, N * wide), BF16),
        ((STEPS, N, 4, J, ORB, cols), BF16),
        ((J, N * wide, 2 * cols), BF16),
        ((ORB + cols, 2 * cols), F32),
        ((ORB + cols, cols), BF16),
        ((cols, cols), BF16),
        ((Q * wide, cols), BF16),
        ((ORB, cols), F32),
        ((ORB, ORB), BF16),
        ((1, ORB), F32),
        ((4, ORB, cols), F32),
        ((4, ORB, J * cols), F32),
        ((STEPS, ORB, cols), BF16),
        ((STEPS, N, ORB, cols), BF16),
        ((STEPS, N, ORB, cols), BF16),
        ((STEPS, J, 3, ORB, 2 * cols), BF16),
        ((STEPS, J, 3, ORB, 2 * cols), BF16),
        ((STEPS, 2, 4, ORB, cols), BF16),
        ((STEPS, Q, 4, ORB, cols), BF16),
        ((4, ORB, cols), BF16),
    ]
    part = (2, J, ORB, cols)
    new = pl.pallas_call(
        functools.partial(kernel, dt),
        out_shape=jax.ShapeDtypeStruct((4, J, ORB, cols), BF16),
        in_specs=[pl.BlockSpec(memory_space=pl.ANY)] * 4,
        out_specs=pl.BlockSpec(memory_space=pltpu.VMEM),
        scratch_shapes=[pltpu.VMEM(shape, dtype) for shape, dtype in buffers] + sems,
        compiler_params=pltpu.CompilerParams(
            collective_id=0, has_side_effects=True, vmem_limit_bytes=56 * 1024 * 1024
        ),
        cost_estimate=pl.CostEstimate(flops=4 * 10**9, bytes_accessed=10**6, transcendentals=0),
    )(lesser.reshape(part), greater.reshape(part), hopping, coupling.reshape(1, ORB))
    new = new.reshape(4, rows, cols)
    return new[:2], new[2:]


def solution(mesh):
    in_specs = (P(None, "trow", "tcol"), P(None, "trow", "tcol"), P(), P())
    out_specs = (P(None, "trow", "tcol"), P(None, "trow", "tcol"))
    return jax.shard_map(per_device, mesh=mesh, in_specs=in_specs, out_specs=out_specs, check_vma=False)
```

```python
import functools

import jax
import jax.numpy as jnp
from jax import lax
from jax.experimental import pallas as pl
from jax.experimental.pallas import tpu as pltpu
from jax.sharding import PartitionSpec as P

MESH = pl.DeviceIdType.MESH
ORB = 32
STEPS = 2
N = 8
Q = 4
Y = 4
J = 3
HALF = ORB // 2
F32 = jnp.float32
BF16 = jnp.bfloat16
NT = (((1,), (1,)), ((), ()))
NN = (((1,), (0,)), ((), ()))
PIECES = ((0, 0, Q * J), (1, 0, Q * J), (2, 0, Q), (2, Q, Q), (2, 2 * Q, Q))


def dot(a, b, dims=NN):
    return lax.dot_general(a, b, dims, preferred_element_type=F32)


def kernel(
    dt, lesser, greater, hopping, coupling, out,
    x, xt, xq, t1, f, sg, hb, bm, acc, pre, eye, gather, w, hm, cv, before, hop, zs_s, zs_r, cs, rs_s, rs_r, ax_s, ax_r, ed,
    s_in, s_t1, r_t1, s_t2, r_t2, s_q, r_q, s_h, r_h, s_g, r_g,
    s_zs, r_zs, s_cs, r_cs, s_rs, r_rs, s_ax, r_ax, s_ed, r_ed,
):
    cols = x.shape[-1]
    wide = 4 * ORB
    r = lax.axis_index("trow")
    b = lax.axis_index("tcol")
    z, q = r // Q, r % Q
    xh, y = b // Y, b % Y

    def at(zz, qq, bb):
        return {"trow": zz * Q + qq, "tcol": bb}

    drains = []

    def drain_now(upto):
        for drain in upto:
            drain()

    def copy_of(src, dst, ss, rs, where):
        return pltpu.make_async_remote_copy(
            src_ref=src, dst_ref=dst, send_sem=ss, recv_sem=rs, device_id=where, device_id_type=MESH
        )

    def push(src, dst, ss, rs, where):
        copy_of(src, dst, ss, rs, where).start()

    def owe(ref, ss):
        drains.append(copy_of(ref, ref, ss, s_in.at[0], at(z, q, b)).wait_send)

    def arrive(ref, rs):
        copy_of(ref, ref, s_in.at[0], rs, at(z, q, b)).wait_recv()

    def place(dx, dy):
        return ((xh + dx) % 2) * Y + (y + dy) % Y

    up, down = at((z + 1) % N, q, b), at((z + N - 1) % N, q, b)


    def mirror_out(st, j):
        k = st * J + j
        for i in range(1, N):
            p = (b + i) % N
            src = x.at[st, p // 2, j, pl.ds(pl.multiple_of(HALF * (p % 2), HALF), HALF)]
            push(src, t1.at[st, j, b], s_t1.at[k], r_t1.at[k], at(z, q, p))
        owe(t1.at[st, j, pl.ds(0, N - 1)], s_t1.at[k])
        t1[st, j, b] = x[st, b // 2, j, pl.ds(pl.multiple_of(HALF * (b % 2), HALF), HALF)]

    def mirror_on(st, j):
        k = st * J + j
        arrive(t1.at[st, j, pl.ds(0, N - 1)], r_t1.at[k])
        for i in range(N):
            bb = (b + N - i) % N
            here = jnp.logical_and(bb == z, b == z)

            @pl.when(jnp.logical_not(here))
            def _():
                push(t1.at[st, j, bb], f.at[st, j, b], s_t2.at[k], r_t2.at[k], at(bb, q, z))

            @pl.when(here)
            def _():
                f[st, j, b] = t1[st, j, bb]

        def drain():
            for n, cond in ((N - 1, b == z), (N, b != z)):
                @pl.when(cond)
                def _():
                    ref = t1.at[st, j, pl.ds(0, n)]
                    copy_of(ref, ref, s_t2.at[k], s_in.at[0], at(z, q, b)).wait_send()

        drains.append(drain)

    def mirror_in(st, j):
        for n, cond in ((N - 1, b == z), (N, b != z)):
            @pl.when(cond)
            def _():
                arrive(f.at[st, j, pl.ds(0, n)], r_t2.at[st * J + j])

    def quad_out(st):
        for c in range(4):
            xt[st, :, c, :, 0:J * ORB] = dot(eye[...], x[st, c].reshape(J * ORB, cols), NT).astype(BF16).reshape(Q, J * ORB, J * ORB)
        lanes = pl.ds(pl.multiple_of(wide * q, wide), wide)
        for j in range(J):
            part = pl.ds(j * ORB, ORB)
            k = st * J + j
            for i in range(1, Q):
                to = (q + i) % Q
                push(xt.at[st, to, :, part], xq.at[st, :, part, lanes], s_q.at[k], r_q.at[k], at(z, to, b))
            owe(xq.at[st, :, part, pl.ds(0, (Q - 1) * wide)], s_q.at[k])
        xq[st, :, :, lanes] = xt[st, q]

    def quad_in(st, j):
        arrive(xq.at[st, :, pl.ds(j * ORB, ORB), pl.ds(0, (Q - 1) * wide)], r_q.at[st * J + j])

    def history(st, s, j):
        k = st * J + j
        lo, hi = (z + N - s) % N, (z + s) % N
        if s > 0:
            arrive(hb.at[st, pl.ds(0, 1 if s == 4 else 2), :, j], r_h.at[4 * k + s - 1])
        if s < 4:
            first, second = (pl.ds(0, 2), pl.ds(2, 2)) if s == 3 else (pl.ds(0, 4), pl.ds(0, 4))
            one, two = hb.at[st, lo, first, j], hb.at[st, hi, second, j]
            from_one, from_two = (x.at[st, :, j], x.at[st, :, j]) if s == 0 else (one, two)
            push(from_one, one, s_h.at[k], r_h.at[4 * k + s], up)
            push(from_two, two, s_h.at[k], r_h.at[4 * k + s], down)
        if s == 3:
            owe(hb.at[st, pl.ds(0, N - 1), :, j], s_h.at[k])

    def tile(st, piece, bb):
        k, m, n = PIECES[piece]
        return sg.at[st, k, pl.ds(ORB * (1 + m), ORB * n), pl.ds(pl.multiple_of(wide * bb, wide), wide)]

    WAIT = (0, 1, 3, 3, 2, 3, 3)

    def several(st, piece, n):
        k, m, rows = PIECES[piece]
        return sg.at[st, k, pl.ds(ORB * (1 + m), ORB * rows), pl.ds(0, n * wide)]

    def give(st, piece, way, bb, to):
        k = st * len(PIECES) + piece
        push(tile(st, piece, bb), tile(st, piece, bb), s_g.at[k], r_g.at[4 * k + WAIT[way]], at(z, q, to))

    def take(st, piece, wait):
        arrive(several(st, piece, 4 if wait == 3 else 1), r_g.at[4 * (st * len(PIECES) + piece) + wait])

    def give_own(st, piece):
        give(st, piece, 0, b, place(1, 0))
        give(st, piece, 1, b, place(0, 1))
        give(st, piece, 2, b, place(0, 3))

    def give_partner(st, piece):
        take(st, piece, 0)
        give(st, piece, 3, place(1, 0), place(0, 1))
        give(st, piece, 4, place(1, 0), place(0, 3))

    def give_far(st, piece):
        take(st, piece, 1)
        give(st, piece, 5, place(0, 3), place(0, 1))

    def give_far_partner(st, piece):
        take(st, piece, 2)
        give(st, piece, 6, place(1, 1), place(0, 3))
        owe(several(st, piece, 7), s_g.at[st * len(PIECES) + piece])

    def take_rest(st, piece):
        take(st, piece, 3)


    into = [
        pltpu.make_async_copy(lesser, x.at[0, pl.ds(0, 2)], s_in.at[1]),
        pltpu.make_async_copy(greater, x.at[0, pl.ds(2, 2)], s_in.at[2]),
        pltpu.make_async_copy(hopping, hm, s_in.at[3]),
        pltpu.make_async_copy(coupling, cv, s_in.at[4]),
    ]
    for copy in into:
        copy.start()
    barrier = pltpu.get_barrier_semaphore()
    for i in range(1, N):
        pl.semaphore_signal(barrier, inc=1, device_id=at((z + i) % N, q, b), device_id_type=MESH)
        pl.semaphore_signal(barrier, inc=1, device_id=at(z, q, (b + i) % N), device_id_type=MESH)
    for i in range(1, Q):
        pl.semaphore_signal(barrier, inc=1, device_id=at(z, (q + i) % Q, b), device_id_type=MESH)
    row = lax.broadcasted_iota(jnp.int32, (ORB + cols, cols), 0) - ORB
    col = lax.broadcasted_iota(jnp.int32, (ORB + cols, cols), 1)
    when = jnp.where(row < 0, Q * J, ((row >> 5) & 3) * J + (row >> 7))
    pre[...] = jnp.where(jnp.logical_and((row & 31) == (col & 31), (col >> 5) < when), 1.0, 0.0).astype(BF16)
    eye[...] = jnp.where(
        lax.broadcasted_iota(jnp.int32, (cols, cols), 0) == lax.broadcasted_iota(jnp.int32, (cols, cols), 1), 1.0, 0.0
    ).astype(BF16)
    from_q = lax.broadcasted_iota(jnp.int32, (Q * wide, cols), 0)
    to_q = lax.broadcasted_iota(jnp.int32, (Q * wide, cols), 1)
    packed = (from_q >> 7) * (J * ORB) + (from_q & 127)
    gather[...] = jnp.where(jnp.logical_and((from_q & 127) < J * ORB, packed == to_q), 1.0, 0.0).astype(BF16)
    xt[...] = jnp.zeros_like(xt)
    for copy in into:
        copy.wait()
    across = jnp.broadcast_to(cv[...], (ORB, ORB))
    same = lax.broadcasted_iota(jnp.int32, (ORB, ORB), 0) == lax.broadcasted_iota(jnp.int32, (ORB, ORB), 1)
    tall = jnp.sum(jnp.where(same, across, 0.0), axis=1, keepdims=True)
    same = lax.broadcasted_iota(jnp.int32, (ORB, cols), 0) == (lax.broadcasted_iota(jnp.int32, (ORB, cols), 1) & 31)
    flat = jnp.sum(jnp.where(same, jnp.broadcast_to(tall, (ORB, cols)), 0.0), axis=0, keepdims=True)
    w[...] = tall * flat

    hb[0, z] = x[0]

    pl.semaphore_wait(barrier, 2 * (N - 1) + Q - 1)

    def build(st, zz):
        got = hb[st, zz]
        rows = pl.ds(pl.multiple_of(wide * zz, wide), wide)
        for j in range(J):
            lr, li, gr, gi = got[0, j], got[1, j], got[2, j], got[3, j]
            bm[j, rows, 0:cols] = jnp.concatenate([lr, -li, -gr, gi], axis=0)
            bm[j, rows, cols:2 * cols] = jnp.concatenate([li, lr, -gi, -gr], axis=0)
        before[...] += jnp.where(zz < z, jnp.sum(got.astype(F32), axis=1), 0.0)

    mirror_out(0, 0)
    history(0, 0, 0)
    history(0, 0, 1)
    history(0, 0, 2)

    mirror_out(0, 1)
    mirror_out(0, 2)
    quad_out(0)

    for st in range(STEPS):
        earlier, drains[:] = list(drains), []
        before[...] = jnp.zeros_like(before)
        mirror_on(st, 0)
        mirror_on(st, 1)
        mirror_on(st, 2)
        history(st, 1, 0)
        history(st, 1, 1)

        for j in range(J):
            quad_in(st, j)
            base = [dot(xq[st, c, j * ORB:(j + 1) * ORB], gather[...]) for c in range(4)]
            mirror_in(st, j)
            mir = f[st, j].reshape(4, ORB, cols).astype(F32)
            weight = w[...]

            def energy(br, bi, mr, mi):
                sr = br * br - bi * bi
                si = 2.0 * br * bi
                return [((sr * mr - si * mi) * weight).astype(BF16), ((sr * mi + si * mr) * weight).astype(BF16)]

            sigma = jnp.concatenate(
                energy(base[2], base[3], mir[0], mir[1]) + energy(base[0], base[1], mir[2], mir[3]),
                axis=0,
            )
            summed = dot(pre[...], sigma, NT).astype(BF16)
            sg[st, j, pl.ds(ORB, cols), pl.ds(pl.multiple_of(wide * b, wide), wide)] = summed[ORB:]
            zs_s[st, :, j * wide:(j + 1) * wide] = summed[:ORB]
            for piece, (k, _, _) in enumerate(PIECES):
                if k == j:
                    give_own(st, piece)
            if j == 0:
                history(st, 1, 2)
            if j == 1:
                history(st, 2, 0)

        for i in range(1, N):
            push(zs_s.at[st], zs_r.at[st, z], s_zs.at[st], r_zs.at[st], at((z + i) % N, q, b))
        owe(zs_r.at[st, pl.ds(0, N - 1)], s_zs.at[st])

        earlier, drains[:] = earlier + drains, []
        history(st, 2, 1)
        build(st, z)
        give_partner(st, 0)
        give_far(st, 0)
        build(st, (z + 1) % N)
        build(st, (z + N - 1) % N)
        give_partner(st, 1)
        give_far(st, 1)
        history(st, 2, 2)
        give_far_partner(st, 0)
        give_partner(st, 2)
        give_far(st, 2)
        carry = jnp.zeros((ORB, cols), F32)
        arrive(zs_r.at[st, pl.ds(0, N - 1)], r_zs.at[st])
        for zz in range(N - 1):
            carry = carry + jnp.where(zz < z, zs_r[st, zz].astype(F32), 0.0)
        cs[st, b] = carry.astype(BF16)
        for i in range(1, N):
            push(cs.at[st, b], cs.at[st, b], s_cs.at[st], r_cs.at[st], at(z, q, (b + i) % N))
        owe(cs.at[st, pl.ds(0, N - 1)], s_cs.at[st])

        history(st, 3, 0)
        give_partner(st, 3)
        give_far(st, 3)
        give_partner(st, 4)
        give_far(st, 4)
        give_far_partner(st, 1)
        history(st, 3, 1)
        build(st, (z + 2) % N)
        build(st, (z + N - 2) % N)
        history(st, 3, 2)
        give_far_partner(st, 2)
        give_far_partner(st, 3)
        give_far_partner(st, 4)
        build(st, (z + 3) % N)
        build(st, (z + N - 3) % N)
        drain_now(earlier)
        for j in range(J):
            history(st, 4, j)
        build(st, (z + 4) % N)

        ax_s[st, 0] = before[...].astype(BF16)
        ax_s[st, 1] = (before[...] + jnp.sum(x[st].astype(F32), axis=1)).astype(BF16)
        sib = (q // 2) * 2 + (1 - q % 2)
        par = (q + 2) % Q
        dia = (sib + 2) % Q
        k = st * 3
        push(ax_s.at[st, 1 - q // 2], ax_r.at[st, q], s_ax.at[st], r_ax.at[k], at(z, par, b))
        push(ax_s.at[st, 1 - q % 2], ax_r.at[st, q], s_ax.at[st], r_ax.at[k + 1], at(z, sib, b))
        if st == 0:
            @pl.when(q == 0)
            def _():
                ed[...] = hb[0, 0, :, 0]
                for i in range(1, Q):
                    push(hb.at[0, 0, :, 0], ed, s_ed.at[0], r_ed.at[0], at(z, i, b))

        arrive(cs.at[st, pl.ds(0, N - 1)], r_cs.at[st])
        for bb in range(N):
            for j in range(J):
                sg[st, j, 0:ORB, bb * wide:(bb + 1) * wide] = cs[st, bb, :, j * wide:(j + 1) * wide]
        take_rest(st, 0)
        acc[...] = dot(sg[st, 0], bm[0])
        take_rest(st, 1)
        acc[...] += dot(sg[st, 1], bm[1])

        def rows_of(m, qq):
            return acc[pl.ds(pl.multiple_of(ORB + m * wide + ORB * qq, ORB), ORB), :]

        def cross(m):
            k = 2 * (st * J + m)
            arrive(rs_r.at[st, m, pl.ds(0, 2)], r_rs.at[k])
            rs_s[st, m, 2] = (rows_of(m, par) + rs_r[st, m, 1].astype(F32)).astype(BF16)
            push(rs_s.at[st, m, 2], rs_r.at[st, m, 2], s_rs.at[k + 1], r_rs.at[k + 1], at(z, par, b))
            owe(rs_s.at[st, m, 2], s_rs.at[k + 1])

        lead = None
        for m in range(J):
            take_rest(st, 2 + m)
            lo, hi = (0 if m == 0 else ORB + m * wide), ORB + (m + 1) * wide
            part = acc[lo:hi, :] + dot(sg[st, 2, lo:hi, :], bm[2])
            if m == 0:
                lead = jnp.concatenate([part[:ORB]] * Q, axis=0)
                part = part[ORB:]
            part = part + lead
            acc[ORB + m * wide:hi, :] = part
            rs_s[st, m, 0] = rows_of(m, sib).astype(BF16)
            rs_s[st, m, 1] = rows_of(m, dia).astype(BF16)
            k = 2 * (st * J + m)
            push(rs_s.at[st, m, pl.ds(0, 2)], rs_r.at[st, m, pl.ds(0, 2)], s_rs.at[k], r_rs.at[k], at(z, sib, b))
            owe(rs_s.at[st, m, pl.ds(0, 2)], s_rs.at[k])
            if m > 0:
                cross(m - 1)
        cross(J - 1)

        level = before[...]
        k = st * 3
        arrive(ax_r.at[st, par], r_ax.at[k])
        push(ax_r.at[st, par], ax_r.at[st, par], s_ax.at[st], r_ax.at[k + 2], at(z, sib, b))
        owe(ax_r.at[st, pl.ds(0, 3)], s_ax.at[st])
        arrive(ax_r.at[st, sib], r_ax.at[k + 1])
        arrive(ax_r.at[st, dia], r_ax.at[k + 2])
        for other in (par, sib, dia):
            level = level + ax_r[st, other].astype(F32)
        for c in range(4):
            run = level[c]
            runs = [run]
            for j in range(J - 1):
                run = run + x[st, c, j].astype(F32)
                runs.append(run)
            run = jnp.concatenate(runs, axis=1)
            high = run.astype(BF16)
            low = (run - high.astype(F32)).astype(BF16)
            hop[c] = dot(hm[...], high) + dot(hm[...], low)
        if st == 0:
            @pl.when(q != 0)
            def _():
                arrive(ed, r_ed.at[0])

            def drain():
                @pl.when(q == 0)
                def _():
                    ref = ax_r.at[0, pl.ds(0, 3)]
                    copy_of(ref, ref, s_ed.at[0], s_in.at[0], at(z, q, b)).wait_send()

            drains.append(drain)
        earlier, drains[:] = list(drains), []
        drain_now(earlier)

        for m in range(J):
            arrive(rs_r.at[st, m, 2], r_rs.at[2 * (st * J + m) + 1])
            coll = rows_of(m, q) + rs_r[st, m, 0].astype(F32) + rs_r[st, m, 2].astype(F32)
            coll = dt * coll
            for c in range(4):
                edge = ed[c].astype(F32)
                lanes = slice(m * cols, (m + 1) * cols)
                if c % 2 == 0:
                    new = edge + dt * (hop[c + 1, :, lanes] + coll[:, cols:])
                else:
                    new = edge - dt * (hop[c - 1, :, lanes] + coll[:, :cols])
                if st + 1 < STEPS:
                    x[st + 1, c, m] = new.astype(BF16)
                else:
                    out[c, m] = new.astype(BF16)
            if st + 1 < STEPS:
                hb[st + 1, z, :, m] = x[st + 1, :, m]
                mirror_out(st + 1, m)
                history(st + 1, 0, m)
        if st + 1 < STEPS:
            quad_out(st + 1)

    drain_now(drains)


def per_device(lesser, greater, hopping, coupling):
    rows, cols = lesser.shape[1:]
    dt = 3.0 / (rows * N * Q // ORB)
    wide = 4 * ORB

    def dma(n):
        return pltpu.SemaphoreType.DMA((n,))

    pieces = STEPS * J
    sems = [dma(5)]
    for sent, got in (
        (pieces, pieces), (pieces, pieces), (pieces, pieces), (pieces, 4 * pieces),
        (STEPS * len(PIECES), STEPS * len(PIECES) * 4), (STEPS, STEPS), (STEPS, STEPS),
        (2 * pieces, 2 * pieces), (STEPS, 3 * STEPS), (1, 1),
    ):
        sems += [dma(sent), dma(got)]
    buffers = [
        ((STEPS, 4, J, ORB, cols), BF16),
        ((STEPS, Q, 4, J * ORB, wide), BF16),
        ((STEPS, 4, J * ORB, Q * wide), BF16),
        ((STEPS, J, N, HALF, cols), BF16),
        ((STEPS, J, N, HALF, cols), BF16),
        ((STEPS, J, ORB + cols, N * wide), BF16),
        ((STEPS, N, 4, J, ORB, cols), BF16),
        ((J, N * wide, 2 * cols), BF16),
        ((ORB + cols, 2 * cols), F32),
        ((ORB + cols, cols), BF16),
        ((cols, cols), BF16),
        ((Q * wide, cols), BF16),
        ((ORB, cols), F32),
        ((ORB, ORB), BF16),
        ((1, ORB), F32),
        ((4, ORB, cols), F32),
        ((4, ORB, J * cols), F32),
        ((STEPS, ORB, cols), BF16),
        ((STEPS, N, ORB, cols), BF16),
        ((STEPS, N, ORB, cols), BF16),
        ((STEPS, J, 3, ORB, 2 * cols), BF16),
        ((STEPS, J, 3, ORB, 2 * cols), BF16),
        ((STEPS, 2, 4, ORB, cols), BF16),
        ((STEPS, Q, 4, ORB, cols), BF16),
        ((4, ORB, cols), BF16),
    ]
    part = (2, J, ORB, cols)
    new = pl.pallas_call(
        functools.partial(kernel, dt),
        out_shape=jax.ShapeDtypeStruct((4, J, ORB, cols), BF16),
        in_specs=[pl.BlockSpec(memory_space=pl.ANY)] * 4,
        out_specs=pl.BlockSpec(memory_space=pltpu.VMEM),
        scratch_shapes=[pltpu.VMEM(shape, dtype) for shape, dtype in buffers] + sems,
        compiler_params=pltpu.CompilerParams(
            collective_id=0, has_side_effects=True, vmem_limit_bytes=56 * 1024 * 1024
        ),
        cost_estimate=pl.CostEstimate(flops=4 * 10**9, bytes_accessed=10**6, transcendentals=0),
    )(lesser.reshape(part), greater.reshape(part), hopping, coupling.reshape(1, ORB))
    new = new.reshape(4, rows, cols)
    return new[:2], new[2:]


def solution(mesh):
    in_specs = (P(None, "trow", "tcol"), P(None, "trow", "tcol"), P(), P())
    out_specs = (P(None, "trow", "tcol"), P(None, "trow", "tcol"))
    return jax.shard_map(per_device, mesh=mesh, in_specs=in_specs, out_specs=out_specs, check_vma=False)
```

```python
import functools

import jax
import jax.numpy as jnp
from jax import lax
from jax.experimental import pallas as pl
from jax.experimental.pallas import tpu as pltpu
from jax.sharding import PartitionSpec as P

MESH = pl.DeviceIdType.MESH
ORB = 32
STEPS = 2
N = 8
Q = 4
Y = 4
J = 3
HALF = ORB // 2
F32 = jnp.float32
BF16 = jnp.bfloat16
NT = (((1,), (1,)), ((), ()))
NN = (((1,), (0,)), ((), ()))
PIECES = ((0, 0, Q * J), (1, 0, Q * J), (2, 0, Q), (2, Q, Q), (2, 2 * Q, Q))


def dot(a, b, dims=NN):
    return lax.dot_general(a, b, dims, preferred_element_type=F32)


def kernel(
    dt, lesser, greater, hopping, coupling, out,
    x, xt, xq, t1, f, sg, hb, bm, acc, pre, eye, gather, w, hm, cv, before, hop, zs_s, zs_r, cs, rs_s, rs_r, ax_s, ax_r, ed,
    s_in, s_t1, r_t1, s_t2, r_t2, s_q, r_q, s_h, r_h, s_g, r_g,
    s_zs, r_zs, s_cs, r_cs, s_rs, r_rs, s_ax, r_ax, s_ed, r_ed,
):
    cols = x.shape[-1]
    wide = 4 * ORB
    r = lax.axis_index("trow")
    b = lax.axis_index("tcol")
    z, q = r // Q, r % Q
    xh, y = b // Y, b % Y

    def at(zz, qq, bb):
        return {"trow": zz * Q + qq, "tcol": bb}

    drains = []

    def drain_now(upto):
        for drain in upto:
            drain()

    def copy_of(src, dst, ss, rs, where):
        return pltpu.make_async_remote_copy(
            src_ref=src, dst_ref=dst, send_sem=ss, recv_sem=rs, device_id=where, device_id_type=MESH
        )

    def push(src, dst, ss, rs, where):
        copy_of(src, dst, ss, rs, where).start()

    def owe(ref, ss):
        drains.append(copy_of(ref, ref, ss, s_in.at[0], at(z, q, b)).wait_send)

    def arrive(ref, rs):
        copy_of(ref, ref, s_in.at[0], rs, at(z, q, b)).wait_recv()

    def place(dx, dy):
        return ((xh + dx) % 2) * Y + (y + dy) % Y

    up, down = at((z + 1) % N, q, b), at((z + N - 1) % N, q, b)


    def mirror_out(st, j):
        k = st * J + j
        for i in range(1, N):
            p = (b + i) % N
            src = x.at[st, p // 2, j, pl.ds(pl.multiple_of(HALF * (p % 2), HALF), HALF)]
            push(src, t1.at[st, j, b], s_t1.at[k], r_t1.at[k], at(z, q, p))
        owe(t1.at[st, j, pl.ds(0, N - 1)], s_t1.at[k])
        t1[st, j, b] = x[st, b // 2, j, pl.ds(pl.multiple_of(HALF * (b % 2), HALF), HALF)]

    def mirror_on(st, j):
        k = st * J + j
        arrive(t1.at[st, j, pl.ds(0, N - 1)], r_t1.at[k])
        for i in range(N):
            bb = (b + N - i) % N
            here = jnp.logical_and(bb == z, b == z)

            @pl.when(jnp.logical_not(here))
            def _():
                push(t1.at[st, j, bb], f.at[st, j, b], s_t2.at[k], r_t2.at[k], at(bb, q, z))

            @pl.when(here)
            def _():
                f[st, j, b] = t1[st, j, bb]

        def drain():
            for n, cond in ((N - 1, b == z), (N, b != z)):
                @pl.when(cond)
                def _():
                    ref = t1.at[st, j, pl.ds(0, n)]
                    copy_of(ref, ref, s_t2.at[k], s_in.at[0], at(z, q, b)).wait_send()

        drains.append(drain)

    def mirror_in(st, j):
        for n, cond in ((N - 1, b == z), (N, b != z)):
            @pl.when(cond)
            def _():
                arrive(f.at[st, j, pl.ds(0, n)], r_t2.at[st * J + j])

    def quad_out(st):
        for c in range(4):
            xt[st, :, c, :, 0:J * ORB] = dot(eye[...], x[st, c].reshape(J * ORB, cols), NT).astype(BF16).reshape(Q, J * ORB, J * ORB)
        lanes = pl.ds(pl.multiple_of(wide * q, wide), wide)
        for j in range(J):
            part = pl.ds(j * ORB, ORB)
            k = st * J + j
            for i in range(1, Q):
                to = (q + i) % Q
                push(xt.at[st, to, :, part], xq.at[st, :, part, lanes], s_q.at[k], r_q.at[k], at(z, to, b))
            owe(xq.at[st, :, part, pl.ds(0, (Q - 1) * wide)], s_q.at[k])
        xq[st, :, :, lanes] = xt[st, q]

    def quad_in(st, j):
        arrive(xq.at[st, :, pl.ds(j * ORB, ORB), pl.ds(0, (Q - 1) * wide)], r_q.at[st * J + j])

    def history(st, s, j):
        k = st * J + j
        lo, hi = (z + N - s) % N, (z + s) % N
        if s > 0:
            arrive(hb.at[st, pl.ds(0, 1 if s == 4 else 2), :, j], r_h.at[4 * k + s - 1])
        if s < 4:
            first, second = (pl.ds(0, 2), pl.ds(2, 2)) if s == 3 else (pl.ds(0, 4), pl.ds(0, 4))
            one, two = hb.at[st, lo, first, j], hb.at[st, hi, second, j]
            from_one, from_two = (x.at[st, :, j], x.at[st, :, j]) if s == 0 else (one, two)
            push(from_one, one, s_h.at[k], r_h.at[4 * k + s], up)
            push(from_two, two, s_h.at[k], r_h.at[4 * k + s], down)
        if s == 3:
            owe(hb.at[st, pl.ds(0, N - 1), :, j], s_h.at[k])

    def tile(st, piece, bb):
        k, m, n = PIECES[piece]
        return sg.at[st, k, pl.ds(ORB * (1 + m), ORB * n), pl.ds(pl.multiple_of(wide * bb, wide), wide)]

    WAIT = (0, 1, 3, 3, 2, 3, 3)

    def several(st, piece, n):
        k, m, rows = PIECES[piece]
        return sg.at[st, k, pl.ds(ORB * (1 + m), ORB * rows), pl.ds(0, n * wide)]

    def give(st, piece, way, bb, to):
        k = st * len(PIECES) + piece
        push(tile(st, piece, bb), tile(st, piece, bb), s_g.at[k], r_g.at[4 * k + WAIT[way]], at(z, q, to))

    def take(st, piece, wait):
        arrive(several(st, piece, 4 if wait == 3 else 1), r_g.at[4 * (st * len(PIECES) + piece) + wait])

    def give_own(st, piece):
        give(st, piece, 0, b, place(1, 0))
        give(st, piece, 1, b, place(0, 1))
        give(st, piece, 2, b, place(0, 3))

    def give_partner(st, piece):
        take(st, piece, 0)
        give(st, piece, 3, place(1, 0), place(0, 1))
        give(st, piece, 4, place(1, 0), place(0, 3))

    def give_far(st, piece):
        take(st, piece, 1)
        give(st, piece, 5, place(0, 3), place(0, 1))

    def give_far_partner(st, piece):
        take(st, piece, 2)
        give(st, piece, 6, place(1, 1), place(0, 3))
        owe(several(st, piece, 7), s_g.at[st * len(PIECES) + piece])

    def take_rest(st, piece):
        take(st, piece, 3)


    into = [
        pltpu.make_async_copy(lesser, x.at[0, pl.ds(0, 2)], s_in.at[1]),
        pltpu.make_async_copy(greater, x.at[0, pl.ds(2, 2)], s_in.at[2]),
        pltpu.make_async_copy(hopping, hm, s_in.at[3]),
        pltpu.make_async_copy(coupling, cv, s_in.at[4]),
    ]
    for copy in into:
        copy.start()
    barrier = pltpu.get_barrier_semaphore()
    for i in range(1, N):
        pl.semaphore_signal(barrier, inc=1, device_id=at((z + i) % N, q, b), device_id_type=MESH)
        pl.semaphore_signal(barrier, inc=1, device_id=at(z, q, (b + i) % N), device_id_type=MESH)
    for i in range(1, Q):
        pl.semaphore_signal(barrier, inc=1, device_id=at(z, (q + i) % Q, b), device_id_type=MESH)
    row = lax.broadcasted_iota(jnp.int32, (ORB + cols, cols), 0) - ORB
    col = lax.broadcasted_iota(jnp.int32, (ORB + cols, cols), 1)
    when = jnp.where(row < 0, Q * J, ((row >> 5) & 3) * J + (row >> 7))
    pre[...] = jnp.where(jnp.logical_and((row & 31) == (col & 31), (col >> 5) < when), 1.0, 0.0).astype(BF16)
    eye[...] = jnp.where(
        lax.broadcasted_iota(jnp.int32, (cols, cols), 0) == lax.broadcasted_iota(jnp.int32, (cols, cols), 1), 1.0, 0.0
    ).astype(BF16)
    from_q = lax.broadcasted_iota(jnp.int32, (Q * wide, cols), 0)
    to_q = lax.broadcasted_iota(jnp.int32, (Q * wide, cols), 1)
    packed = (from_q >> 7) * (J * ORB) + (from_q & 127)
    gather[...] = jnp.where(jnp.logical_and((from_q & 127) < J * ORB, packed == to_q), 1.0, 0.0).astype(BF16)
    xt[...] = jnp.zeros_like(xt)
    for copy in into:
        copy.wait()
    across = jnp.broadcast_to(cv[...], (ORB, ORB))
    same = lax.broadcasted_iota(jnp.int32, (ORB, ORB), 0) == lax.broadcasted_iota(jnp.int32, (ORB, ORB), 1)
    tall = jnp.sum(jnp.where(same, across, 0.0), axis=1, keepdims=True)
    same = lax.broadcasted_iota(jnp.int32, (ORB, cols), 0) == (lax.broadcasted_iota(jnp.int32, (ORB, cols), 1) & 31)
    flat = jnp.sum(jnp.where(same, jnp.broadcast_to(tall, (ORB, cols)), 0.0), axis=0, keepdims=True)
    w[...] = tall * flat

    hb[0, z] = x[0]

    pl.semaphore_wait(barrier, 2 * (N - 1) + Q - 1)

    def build(st, zz):
        got = hb[st, zz]
        rows = pl.ds(pl.multiple_of(wide * zz, wide), wide)
        for j in range(J):
            lr, li, gr, gi = got[0, j], got[1, j], got[2, j], got[3, j]
            bm[j, rows, 0:cols] = jnp.concatenate([lr, -li, -gr, gi], axis=0)
            bm[j, rows, cols:2 * cols] = jnp.concatenate([li, lr, -gi, -gr], axis=0)
        before[...] += jnp.where(zz < z, jnp.sum(got.astype(F32), axis=1), 0.0)

    mirror_out(0, 0)
    history(0, 0, 0)
    history(0, 0, 1)
    history(0, 0, 2)

    mirror_out(0, 1)
    mirror_out(0, 2)
    quad_out(0)

    for st in range(STEPS):
        earlier, drains[:] = list(drains), []
        before[...] = jnp.zeros_like(before)
        mirror_on(st, 0)
        mirror_on(st, 1)
        mirror_on(st, 2)
        history(st, 1, 0)
        history(st, 1, 1)

        for j in range(J):
            quad_in(st, j)
            base = [dot(xq[st, c, j * ORB:(j + 1) * ORB], gather[...]) for c in range(4)]
            mirror_in(st, j)
            mir = f[st, j].reshape(4, ORB, cols).astype(F32)
            weight = w[...]

            def energy(br, bi, mr, mi):
                sr = br * br - bi * bi
                si = 2.0 * br * bi
                return [((sr * mr - si * mi) * weight).astype(BF16), ((sr * mi + si * mr) * weight).astype(BF16)]

            sigma = jnp.concatenate(
                energy(base[2], base[3], mir[0], mir[1]) + energy(base[0], base[1], mir[2], mir[3]),
                axis=0,
            )
            summed = dot(pre[...], sigma, NT).astype(BF16)
            sg[st, j, pl.ds(ORB, cols), pl.ds(pl.multiple_of(wide * b, wide), wide)] = summed[ORB:]
            zs_s[st, :, j * wide:(j + 1) * wide] = summed[:ORB]
            for piece, (k, _, _) in enumerate(PIECES):
                if k == j:
                    give_own(st, piece)
            if j == 0:
                history(st, 1, 2)
            if j == 1:
                history(st, 2, 0)

        for i in range(1, N):
            push(zs_s.at[st], zs_r.at[st, z], s_zs.at[st], r_zs.at[st], at((z + i) % N, q, b))
        owe(zs_r.at[st, pl.ds(0, N - 1)], s_zs.at[st])

        earlier, drains[:] = earlier + drains, []
        history(st, 2, 1)
        build(st, z)
        give_partner(st, 0)
        give_far(st, 0)
        build(st, (z + 1) % N)
        build(st, (z + N - 1) % N)
        give_partner(st, 1)
        give_far(st, 1)
        history(st, 2, 2)
        give_far_partner(st, 0)
        give_partner(st, 2)
        give_far(st, 2)
        carry = jnp.zeros((ORB, cols), F32)
        arrive(zs_r.at[st, pl.ds(0, N - 1)], r_zs.at[st])
        for zz in range(N - 1):
            carry = carry + jnp.where(zz < z, zs_r[st, zz].astype(F32), 0.0)
        cs[st, b] = carry.astype(BF16)
        for i in range(1, N):
            push(cs.at[st, b], cs.at[st, b], s_cs.at[st], r_cs.at[st], at(z, q, (b + i) % N))
        owe(cs.at[st, pl.ds(0, N - 1)], s_cs.at[st])

        history(st, 3, 0)
        give_partner(st, 3)
        give_far(st, 3)
        give_partner(st, 4)
        give_far(st, 4)
        give_far_partner(st, 1)
        history(st, 3, 1)
        build(st, (z + 2) % N)
        build(st, (z + N - 2) % N)
        history(st, 3, 2)
        give_far_partner(st, 2)
        give_far_partner(st, 3)
        give_far_partner(st, 4)
        build(st, (z + 3) % N)
        build(st, (z + N - 3) % N)
        drain_now(earlier)
        for j in range(J):
            history(st, 4, j)
        build(st, (z + 4) % N)

        ax_s[st, 0] = before[...].astype(BF16)
        ax_s[st, 1] = (before[...] + jnp.sum(x[st].astype(F32), axis=1)).astype(BF16)
        sib = (q // 2) * 2 + (1 - q % 2)
        par = (q + 2) % Q
        dia = (sib + 2) % Q
        k = st * 3
        push(ax_s.at[st, 1 - q // 2], ax_r.at[st, q], s_ax.at[st], r_ax.at[k], at(z, par, b))
        push(ax_s.at[st, 1 - q % 2], ax_r.at[st, q], s_ax.at[st], r_ax.at[k + 1], at(z, sib, b))
        if st == 0:
            @pl.when(q == 0)
            def _():
                ed[...] = hb[0, 0, :, 0]
                for i in range(1, Q):
                    push(hb.at[0, 0, :, 0], ed, s_ed.at[0], r_ed.at[0], at(z, i, b))

        arrive(cs.at[st, pl.ds(0, N - 1)], r_cs.at[st])
        for bb in range(N):
            for j in range(J):
                sg[st, j, 0:ORB, bb * wide:(bb + 1) * wide] = cs[st, bb, :, j * wide:(j + 1) * wide]
        take_rest(st, 0)
        acc[...] = dot(sg[st, 0], bm[0])
        take_rest(st, 1)
        acc[...] += dot(sg[st, 1], bm[1])

        def rows_of(m, qq):
            return acc[pl.ds(pl.multiple_of(ORB + m * wide + ORB * qq, ORB), ORB), :]

        def cross(m):
            k = 2 * (st * J + m)
            arrive(rs_r.at[st, m, pl.ds(0, 2)], r_rs.at[k])
            rs_s[st, m, 2] = (rows_of(m, par) + rs_r[st, m, 1].astype(F32)).astype(BF16)
            push(rs_s.at[st, m, 2], rs_r.at[st, m, 2], s_rs.at[k + 1], r_rs.at[k + 1], at(z, par, b))
            owe(rs_s.at[st, m, 2], s_rs.at[k + 1])

        settled, drains[:] = list(drains), []
        lead = None
        for m in range(J):
            take_rest(st, 2 + m)
            lo, hi = (0 if m == 0 else ORB + m * wide), ORB + (m + 1) * wide
            part = acc[lo:hi, :] + dot(sg[st, 2, lo:hi, :], bm[2])
            if m == 0:
                lead = jnp.concatenate([part[:ORB]] * Q, axis=0)
                part = part[ORB:]
            part = part + lead
            acc[ORB + m * wide:hi, :] = part
            rs_s[st, m, 0] = rows_of(m, sib).astype(BF16)
            rs_s[st, m, 1] = rows_of(m, dia).astype(BF16)
            k = 2 * (st * J + m)
            push(rs_s.at[st, m, pl.ds(0, 2)], rs_r.at[st, m, pl.ds(0, 2)], s_rs.at[k], r_rs.at[k], at(z, sib, b))
            owe(rs_s.at[st, m, pl.ds(0, 2)], s_rs.at[k])
            if m > 0:
                cross(m - 1)
        cross(J - 1)

        level = before[...]
        k = st * 3
        arrive(ax_r.at[st, par], r_ax.at[k])
        push(ax_r.at[st, par], ax_r.at[st, par], s_ax.at[st], r_ax.at[k + 2], at(z, sib, b))
        owe(ax_r.at[st, pl.ds(0, 3)], s_ax.at[st])
        arrive(ax_r.at[st, sib], r_ax.at[k + 1])
        arrive(ax_r.at[st, dia], r_ax.at[k + 2])
        for other in (par, sib, dia):
            level = level + ax_r[st, other].astype(F32)
        for c in range(4):
            run = level[c]
            runs = [run]
            for j in range(J - 1):
                run = run + x[st, c, j].astype(F32)
                runs.append(run)
            run = jnp.concatenate(runs, axis=1)
            high = run.astype(BF16)
            low = (run - high.astype(F32)).astype(BF16)
            hop[c] = dot(hm[...], high) + dot(hm[...], low)
        if st == 0:
            @pl.when(q != 0)
            def _():
                arrive(ed, r_ed.at[0])

            def drain():
                @pl.when(q == 0)
                def _():
                    ref = ax_r.at[0, pl.ds(0, 3)]
                    copy_of(ref, ref, s_ed.at[0], s_in.at[0], at(z, q, b)).wait_send()

            drains.append(drain)
        drain_now(settled)

        for m in range(J):
            arrive(rs_r.at[st, m, 2], r_rs.at[2 * (st * J + m) + 1])
            coll = rows_of(m, q) + rs_r[st, m, 0].astype(F32) + rs_r[st, m, 2].astype(F32)
            coll = dt * coll
            for c in range(4):
                edge = ed[c].astype(F32)
                lanes = slice(m * cols, (m + 1) * cols)
                if c % 2 == 0:
                    new = edge + dt * (hop[c + 1, :, lanes] + coll[:, cols:])
                else:
                    new = edge - dt * (hop[c - 1, :, lanes] + coll[:, :cols])
                if st + 1 < STEPS:
                    x[st + 1, c, m] = new.astype(BF16)
                else:
                    out[c, m] = new.astype(BF16)
            if st + 1 < STEPS:
                hb[st + 1, z, :, m] = x[st + 1, :, m]
                mirror_out(st + 1, m)
                history(st + 1, 0, m)
        if st + 1 < STEPS:
            quad_out(st + 1)

    drain_now(drains)


def per_device(lesser, greater, hopping, coupling):
    rows, cols = lesser.shape[1:]
    dt = 3.0 / (rows * N * Q // ORB)
    wide = 4 * ORB

    def dma(n):
        return pltpu.SemaphoreType.DMA((n,))

    pieces = STEPS * J
    sems = [dma(5)]
    for sent, got in (
        (pieces, pieces), (pieces, pieces), (pieces, pieces), (pieces, 4 * pieces),
        (STEPS * len(PIECES), STEPS * len(PIECES) * 4), (STEPS, STEPS), (STEPS, STEPS),
        (2 * pieces, 2 * pieces), (STEPS, 3 * STEPS), (1, 1),
    ):
        sems += [dma(sent), dma(got)]
    buffers = [
        ((STEPS, 4, J, ORB, cols), BF16),
        ((STEPS, Q, 4, J * ORB, wide), BF16),
        ((STEPS, 4, J * ORB, Q * wide), BF16),
        ((STEPS, J, N, HALF, cols), BF16),
        ((STEPS, J, N, HALF, cols), BF16),
        ((STEPS, J, ORB + cols, N * wide), BF16),
        ((STEPS, N, 4, J, ORB, cols), BF16),
        ((J, N * wide, 2 * cols), BF16),
        ((ORB + cols, 2 * cols), F32),
        ((ORB + cols, cols), BF16),
        ((cols, cols), BF16),
        ((Q * wide, cols), BF16),
        ((ORB, cols), F32),
        ((ORB, ORB), BF16),
        ((1, ORB), F32),
        ((4, ORB, cols), F32),
        ((4, ORB, J * cols), F32),
        ((STEPS, ORB, cols), BF16),
        ((STEPS, N, ORB, cols), BF16),
        ((STEPS, N, ORB, cols), BF16),
        ((STEPS, J, 3, ORB, 2 * cols), BF16),
        ((STEPS, J, 3, ORB, 2 * cols), BF16),
        ((STEPS, 2, 4, ORB, cols), BF16),
        ((STEPS, Q, 4, ORB, cols), BF16),
        ((4, ORB, cols), BF16),
    ]
    part = (2, J, ORB, cols)
    new = pl.pallas_call(
        functools.partial(kernel, dt),
        out_shape=jax.ShapeDtypeStruct((4, J, ORB, cols), BF16),
        in_specs=[pl.BlockSpec(memory_space=pl.ANY)] * 4,
        out_specs=pl.BlockSpec(memory_space=pltpu.VMEM),
        scratch_shapes=[pltpu.VMEM(shape, dtype) for shape, dtype in buffers] + sems,
        compiler_params=pltpu.CompilerParams(
            collective_id=0, has_side_effects=True, vmem_limit_bytes=56 * 1024 * 1024
        ),
        cost_estimate=pl.CostEstimate(flops=4 * 10**9, bytes_accessed=10**6, transcendentals=0),
    )(lesser.reshape(part), greater.reshape(part), hopping, coupling.reshape(1, ORB))
    new = new.reshape(4, rows, cols)
    return new[:2], new[2:]


def solution(mesh):
    in_specs = (P(None, "trow", "tcol"), P(None, "trow", "tcol"), P(), P())
    out_specs = (P(None, "trow", "tcol"), P(None, "trow", "tcol"))
    return jax.shard_map(per_device, mesh=mesh, in_specs=in_specs, out_specs=out_specs, check_vma=False)
```
